128 devices in a mesh: section: 2 (over core), peer: 64 (over y, x, z).
Axes of the slice: x: 4, y: 4, z: 4, core: 2. Of those that a mesh axis runs over, the one named last changes fastest.
Arguments:
- inputs: bfloat16 [8192, 5120], P('peer'), may hold values from -6 to 6
- routes: int32 [8192, 1], P('peer'), may hold values from 0 to 63; in each aligned block of 128 rows (0 to 127, 128 to 255, ...) at most 4 rows name the same one
- counts: int32 [64], P('peer'), may hold values from 96 to 128, as said below
- cotangent: bfloat16 [64, 256, 5120], P('peer'), may hold values from -6 to 6
- gain_vector: float32 [2, 5120], P('section'), may hold values from 0.1 to 1.9
- w_down: bfloat16 [2, 5120, 256], P('section'), may hold values from -0.078125 to 0.078125
- w_up: bfloat16 [2, 256, 5120], P('section'), may hold values from -0.375 to 0.375
Outputs:
- grad_gain: bfloat16 [2, 5120], P('section')
- grad_down: bfloat16 [2, 5120, 256], P('section')
- grad_up: bfloat16 [2, 256, 5120], P('section')
- row_grads: bfloat16 [2, 8192, 5120], P('section', 'peer')
The draws below stay inside these ranges and needn't reach their ends.
Inputs may be any that keep to these rules, and one draw needn't show every extreme that they name: `routes`: in the 128 rows of each first-section peer, no destination is named by more than 4 rows, and one is named by exactly 4. `counts`: some peer has all 128 rows live.
All inputs are finite; a program needn't handle non-finite values.
Results may differ from the reference program's by a relative error of at most 0.009.
Values may be sent and summed in bfloat16 or wider, within the bound.
A program may use at most 128 MiB of HBM per device.

```python
import math
import jax
import jax.numpy as jnp
import numpy as np
from jax import lax

D = 5120
R = 256
TOK_DEV = 128
CAP = 4
TOKENS = 8192
N_PEER = 64


def draw_counts(key, part):
    key = jax.random.fold_in(key, 7)
    key_low, key_pick = jax.random.split(key)
    lowest = 3 * TOK_DEV // 4
    counts_drawn = jax.random.randint(key_low, (N_PEER,), lowest, TOK_DEV + 1)
    top_peer = jax.random.randint(key_pick, (), 0, N_PEER)
    counts_drawn = counts_drawn.at[top_peer].set(TOK_DEV)
    counts_drawn = counts_drawn.at[(top_peer + 1) % N_PEER].set(lowest)
    return counts_drawn.astype(jnp.int32)


def block_scale(stream_key, extent, cuts, smallest, top_value):
    gain, own = 1.0, jax.random.fold_in(stream_key, 6)
    for position, parts in cuts:
        heights = jnp.exp(jax.random.uniform(jax.random.fold_in(own, position), (parts,), jnp.float32, smallest / len(cuts), top_value / len(cuts)))
        gain = gain * jnp.repeat(heights, extent[position] // parts).reshape([-1 if axis == position else 1 for axis in range(len(extent))])
    return gain


def routed_block(key, own, number, rows, count, top, reach, skew):
    ranking = jax.random.permutation(key, count)
    heavy_load, ordinary = load_shares(count, rows * top, reach, skew, True), load_shares(count, rows * top, reach, skew, False)
    places = jnp.arange(count)

    def named(lengths, rotation):
        used = int((lengths > 0).sum())
        fixed = max(1, used // 4)
        passed = fixed + (places - fixed + rotation * (used - fixed)) % max(1, count - fixed)
        return jnp.zeros((count,), jnp.int32).at[ranking[jnp.where(places < fixed, places, passed)]].set(jnp.asarray(lengths, jnp.int32))

    lengths = jnp.where(number % 4 == 0, named(heavy_load, number // 4), named(ordinary, number - number // 4 - 1))
    mixed = jax.random.permutation(jax.random.fold_in(own, 3), count)
    giver, sink = mixed[0:count // 2 * 2:2], mixed[1:count // 2 * 2:2]
    room = jnp.minimum(lengths[giver] - 1, reach - lengths[sink]) // 2
    room = jnp.where((giver == ranking[0]) | (sink == ranking[0]) | (lengths[sink] == 0), 0, jnp.maximum(room, 0))
    passed = jax.random.randint(jax.random.fold_in(own, 4), (count // 2,), 0, 1 << 20) % (room + 1)
    lengths = lengths.at[giver].add(-passed).at[sink].add(passed)
    members = jnp.searchsorted(jnp.cumsum(lengths), jnp.arange(rows * top), side="right").astype(jnp.int32)
    listing = members.reshape(top, rows).T
    listing = listing[jax.random.permutation(jax.random.fold_in(own, 1), rows)]
    rotation = jax.random.randint(jax.random.fold_in(own, 2), (rows, 1), 0, top)
    return jnp.take_along_axis(listing, (jnp.arange(top)[None, :] + rotation) % top, axis=1)


def load_shares(amount, total, bound, skew, full):
    weights = [(1 << 20) // math.isqrt(grade ** skew) + 1 for grade in range(1, amount + 1)]
    largest = bound if full else min(bound, max(-(-total // amount), total * weights[0] // sum(weights)))
    least = 1 if total - largest >= amount - 1 else 0
    given, rest = [largest] + [least] * (amount - 1), total - largest - least * (amount - 1)
    while rest > 0:
        movable = [i for i in range(1, amount) if given[i] < largest] or [i for i in range(1, amount) if given[i] < bound]
        whole, budget = sum([weights[i] for i in movable]), rest
        for i in movable:
            more = min(bound - given[i], max(1, budget * weights[i] // whole), rest)
            given[i] = given[i] + more
            rest = rest - more
    return np.array(given)


def normal_values(key, shape, deviation, most, cuts=(), held_as=jnp.bfloat16):
    values = jax.random.normal(key, shape, jnp.float32) * deviation
    if len(cuts) > 0:
        values = block_scale(key, shape, cuts, -0.22, 0.18) * values
    return jnp.clip(values, min=-most, max=most).astype(held_as)


def setup_inputs(seed: int = 0) -> dict:
    splits = jax.random.split(jax.random.key(seed), 8)
    inputs = normal_values(splits[0], (TOKENS, D), 1.0, 6.0, ((0, 64),))
    routes_keys = jax.random.split(jax.random.fold_in(splits[1], 1), TOKENS // TOK_DEV)
    routes_turns = jax.random.permutation(jax.random.fold_in(splits[1], 3), TOKENS // TOK_DEV)
    routes = jax.vmap(lambda own, number: routed_block(jax.random.fold_in(splits[1], 2), own, number, TOK_DEV, N_PEER, 1, CAP, 2))(routes_keys, routes_turns).reshape((TOKENS, 1))
    counts = draw_counts(jax.random.fold_in(splits[7], 71), 0)
    cotangent = normal_values(splits[3], (N_PEER, N_PEER * CAP, D), 1.0, 6.0, ((0, 64),))
    gain_vector = jnp.clip(1.0 + 0.18 * jax.random.normal(splits[4], (2, D), jnp.float32), 0.1, 1.9)
    w_down = normal_values(splits[5], (2, D, R), D ** -0.5, 0.078125, ((0, 2),))
    w_up = normal_values(splits[6], (2, R, D), R ** -0.5, 0.375, ((0, 2),))
    return dict(inputs=inputs, routes=routes, counts=counts, cotangent=cotangent, gain_vector=gain_vector, w_down=w_down, w_up=w_up)


rms_eps = 1e-05

def layer_forward(rows_in, gain_vec, down_w, up_w):
    x_float = rows_in.astype(jnp.float32)
    inv_rms = lax.rsqrt(lax.optimization_barrier(jnp.mean(x_float * x_float, axis=-1, keepdims=True)) + rms_eps)
    x_hat = x_float * inv_rms
    normed = (x_hat * gain_vec).astype(jnp.bfloat16)
    hidden = jnp.dot(normed, down_w, preferred_element_type=jnp.float32)
    active = jax.nn.silu(hidden).astype(jnp.bfloat16)
    result = (x_float + jnp.dot(active, up_w, preferred_element_type=jnp.float32)).astype(jnp.bfloat16)
    return (result, (x_hat, inv_rms, normed, hidden, active))

def layer_backward(saved_state, grad_out, gain_vec, down_w, up_w):
    x_hat, inv_rms, normed, hidden, active = saved_state
    outer = (((0,), (0,)), ((), ()))
    inner = (((1,), (1,)), ((), ()))
    g_up = lax.dot_general(active, grad_out, outer, preferred_element_type=jnp.float32)
    d_active = lax.dot_general(grad_out, up_w, inner, preferred_element_type=jnp.float32)
    gate_sig = jax.nn.sigmoid(hidden)
    d_hidden = (d_active * gate_sig * (1.0 + hidden * (1.0 - gate_sig))).astype(jnp.bfloat16)
    g_down = lax.dot_general(normed, d_hidden, outer, preferred_element_type=jnp.float32)
    d_normed = lax.dot_general(d_hidden, down_w, inner, preferred_element_type=jnp.float32)
    g_gain = lax.optimization_barrier(jnp.sum(d_normed * x_hat, axis=0))
    d_hat = d_normed * gain_vec
    d_input = grad_out.astype(jnp.float32) + inv_rms * (d_hat - x_hat * lax.optimization_barrier(jnp.mean(d_hat * x_hat, axis=-1, keepdims=True)))
    return ((g_gain, g_down, g_up), d_input.astype(jnp.bfloat16))

def reference(inputs, routes, counts, cotangent, gain_vector, w_down, w_up):
    dest_peer = routes[:, 0].reshape(N_PEER, TOK_DEV)
    live_rows = jnp.arange(TOK_DEV, dtype=jnp.int32)[None, :] < counts[:, None]
    one_hot = ((dest_peer[:, :, None] == jnp.arange(N_PEER, dtype=jnp.int32)[None, None, :]) & live_rows[:, :, None]).astype(jnp.int32)
    row_ranks = jnp.cumsum(one_hot, axis=1) - 1
    slot_index = lax.optimization_barrier(jnp.sum(one_hot * row_ranks, axis=-1)) + jnp.arange(N_PEER, dtype=jnp.int32)[:, None] * CAP
    picked = cotangent[dest_peer.reshape(-1), slot_index.reshape(-1)]
    row_cot = jnp.where(live_rows.reshape(-1)[:, None], picked, jnp.zeros_like(picked))
    first_out, saved_first = layer_forward(inputs, gain_vector[0], w_down[0], w_up[0])
    second_out, saved_second = layer_forward(first_out, gain_vector[1], w_down[1], w_up[1])
    grads_second, back_rows = layer_backward(saved_second, row_cot, gain_vector[1], w_down[1], w_up[1])
    grads_first, in_rows = layer_backward(saved_first, back_rows, gain_vector[0], w_down[0], w_up[0])
    factor = float(N_PEER * TOK_DEV) ** (-0.5)
    stacked = [(jnp.stack([a, b]) * factor).astype(jnp.bfloat16) for a, b in zip(grads_first, grads_second)]
    return (stacked[0], stacked[1], stacked[2], jnp.stack([in_rows, back_rows]))
```

```python
import jax
import jax.numpy as jnp
from jax import lax
from jax.experimental import pallas as pl
from jax.experimental.pallas import tpu as pltpu
from jax.sharding import PartitionSpec as P

rms_eps = 1e-05
MESH = pl.DeviceIdType.MESH
BF = jnp.bfloat16
F32 = jnp.float32

ROWS, D, R = 128, 5120, 256
SLOTS, CAP = 256, 4
N_PEER, RING = 64, 4
HALF = D // 2
QUART = HALF // 4
CH = 640
N_CH = D // CH
ACOL = D // RING
UP_OFF, UP_W = (0, 384, 768), (384, 384, 512)
DN_OFF, DN_H = (0, 32, 64), (32, 32, 16)
ORDER = ((0, 1, 2), (1, 2, 0), (2, 0, 1))
FACTOR = float(N_PEER * ROWS) ** (-0.5)
INNER = (((1,), (1,)), ((), ()))


def mod4(v):
    return lax.rem(v + 8, 4)


def rcopy(src, dst, send_sem, recv_sem, device):
    return pltpu.make_async_remote_copy(
        src_ref=src,
        dst_ref=dst,
        send_sem=send_sem,
        recv_sem=recv_sem,
        device_id=device,
        device_id_type=MESH,
    )


def wait_recv(dst, sems, device):
    rcopy(dst, dst, sems[0], sems[1], device).wait_recv()


def wait_send(src, sems, device):
    rcopy(src, src, sems[0], sems[1], device).wait_send()


def kernel(
    x_hbm, routes_ref, counts_ref, cot_hbm, gain_ref, wd_hbm, wu_hbm,
    out_gain, out_dn, out_up, out_rows,
    x_v, wd_v, wu_v, cot_v, a2a_send, a2a_recv, nt, cv, fo, sel, act_t,
    gu0, gu1, gu2, gd0, gd1, gd2,
    ru0, ru1, ru2, rd0, rd1, rd2,
    iu0, iu1, iu2, id0, id1, id2,
    su0, su1, su2, sd0, sd1, sd2,
    i2u0, i2u1, i2u2, i2d0, i2d1, i2d2,
    s2u0, s2u1, s2u2, s2d0, s2d1, s2d2,
    i3u0, i3u1, i3u2, i3d0, i3d1, i3d2,
    gg, gin,
    load_sem, own_sem, a2a_ssem, a2a_rsem, row_ssem, row_rsem, red_ssem, red_rsem, gain_ssem, gain_rsem,
):
    grad = ((gu0, gu1, gu2), (gd0, gd1, gd2))
    rly = ((ru0, ru1, ru2), (rd0, rd1, rd2))
    inb = ((iu0, iu1, iu2), (id0, id1, id2))
    s1 = ((su0, su1, su2), (sd0, sd1, sd2))
    in2 = ((i2u0, i2u1, i2u2), (i2d0, i2d1, i2d2))
    s2 = ((s2u0, s2u1, s2u2), (s2d0, s2d1, s2d2))
    in3 = ((i3u0, i3u1, i3u2), (i3d0, i3d1, i3d2))

    sec = lax.axis_index("section")
    me = lax.axis_index("peer")
    pos = (me // 16, lax.rem(me // 4, 4), lax.rem(me, 4))
    weight = (16, 4, 1)

    def along(axis, step):
        there = mod4(pos[axis] + step)
        return (sec, me + (there - pos[axis]) * weight[axis])

    partner = (1 - sec, me)

    cot_load = pltpu.make_async_copy(
        cot_hbm.at[0, :, pl.ds(pl.multiple_of(sec * HALF, HALF), HALF)], cot_v, load_sem.at[0]
    )
    wd_load = pltpu.make_async_copy(wd_hbm.at[0], wd_v, load_sem.at[1])
    wu_load = pltpu.make_async_copy(wu_hbm.at[0], wu_v, load_sem.at[2])
    x_load = pltpu.make_async_copy(x_hbm, x_v, load_sem.at[3])
    cot_load.start()

    @pl.when(sec == 0)
    def _():
        x_load.start()

    wd_load.start()
    wu_load.start()

    barrier = pltpu.get_barrier_semaphore()

    @pl.when(sec == 0)
    def _():
        pl.semaphore_signal(barrier, inc=1, device_id=partner, device_id_type=MESH)
        for axis in range(3):
            for step in range(1, 4):
                pl.semaphore_signal(barrier, inc=1, device_id=along(axis, step), device_id_type=MESH)

    @pl.when(sec == 1)
    def _():
        def greet(i, carry):
            pl.semaphore_signal(
                barrier, inc=1, device_id=(sec, lax.rem(me + i, N_PEER)), device_id_type=MESH
            )
            return carry

        lax.fori_loop(1, N_PEER, greet, 0)

    cot_load.wait()
    o_i = lax.broadcasted_iota(jnp.int32, (SLOTS, SLOTS), 0)
    i_i = lax.broadcasted_iota(jnp.int32, (SLOTS, SLOTS), 1)
    perm = jnp.where(i_i == (o_i & 3) * 64 + (o_i >> 2), 1.0, 0.0).astype(BF)

    def arrange(g, carry):
        rows = pl.ds(pl.multiple_of(g * 64, 64), 64)
        block = jnp.concatenate(
            [cot_v[rows, j * QUART:(j + 1) * QUART] for j in range(4)], axis=0
        )
        moved = jnp.dot(perm, block, preferred_element_type=F32).astype(BF)
        a2a_send[pl.ds(pl.multiple_of(g * 16, 16), 16)] = moved.reshape(16, 16, QUART)
        return carry

    lax.fori_loop(0, 4, arrange, 0)

    @pl.when(sec == 0)
    def _():
        pl.semaphore_wait(barrier, 10)

        def send(i, carry):
            dst = lax.rem(me + i * 21, N_PEER)
            rcopy(
                a2a_send.at[dst], a2a_recv.at[0, me], a2a_ssem, a2a_rsem.at[0], (1, dst)
            ).start()
            return carry

        lax.fori_loop(0, N_PEER, send, 0)

    @pl.when(sec == 1)
    def _():
        pl.semaphore_wait(barrier, N_PEER)
        pl.semaphore_signal(barrier, inc=1, device_id=partner, device_id_type=MESH)
        pltpu.make_async_copy(a2a_send.at[me], a2a_recv.at[1, me], own_sem).start()

        def send(i, carry):
            dst = lax.rem(me + i * 21, N_PEER)
            rcopy(
                a2a_send.at[dst], a2a_recv.at[1, me], a2a_ssem, a2a_rsem.at[1], (1, dst)
            ).start()
            return carry

        lax.fori_loop(1, N_PEER, send, 0)

    def cols_of(c):
        return pl.ds(pl.multiple_of(c * CH, CH), CH)

    def row_wait(ref, c):
        return rcopy(ref.at[:, cols_of(c)], ref.at[:, cols_of(c)], row_ssem.at[c], row_rsem.at[c], partner)

    @pl.when(sec == 0)
    def _():
        x_load.wait()

    def squares(c, total):
        @pl.when(sec == 1)
        def _():
            row_wait(x_v, c).wait_recv()

        xf = x_v[:, cols_of(c)].astype(F32)
        return total + jnp.sum(xf * xf, axis=1, keepdims=True)

    total = lax.fori_loop(0, N_CH, squares, jnp.zeros((ROWS, 1), F32))
    inv = lax.rsqrt(total / D + rms_eps)
    wd_load.wait()

    def down(c, hidden):
        xf = x_v[:, cols_of(c)].astype(F32)
        normed = (xf * inv * gain_ref[:, cols_of(c)]).astype(BF)
        nt[c // 2, pl.ds(pl.multiple_of(lax.rem(c, 2) * 8, 8), 8)] = normed.T.reshape(8, 80, ROWS)
        return hidden + jnp.dot(normed, wd_v[cols_of(c), :], preferred_element_type=F32)

    hidden = lax.fori_loop(0, N_CH, down, jnp.zeros((ROWS, R), F32))
    gate = jax.nn.sigmoid(hidden)
    active = (hidden * gate).astype(BF)
    act_t[...] = active.T
    wu_load.wait()

    @pl.when(sec == 0)
    def _():
        def up(c, carry):
            y = jnp.dot(active, wu_v[:, cols_of(c)], preferred_element_type=F32)
            fo[:, cols_of(c)] = (x_v[:, cols_of(c)].astype(F32) + y).astype(BF)
            rcopy(
                fo.at[:, cols_of(c)], x_v.at[:, cols_of(c)], row_ssem.at[c], row_rsem.at[c], partner
            ).start()
            return carry

        lax.fori_loop(0, N_CH, up, 0)

    @pl.when(sec == 1)
    def _():
        dest = routes_ref[...]
        live = lax.broadcasted_iota(jnp.int32, (ROWS, 1), 0) < counts_ref[...]
        lane = lax.broadcasted_iota(jnp.int32, (ROWS, ROWS), 1)
        row = lax.broadcasted_iota(jnp.int32, (ROWS, ROWS), 0)
        named = jnp.where((lane == dest) & live, 1.0, 0.0)
        before = jnp.where(lane < row, 1.0, 0.0).astype(BF)
        rank = jnp.dot(before, named.astype(BF), preferred_element_type=F32)
        nth = jnp.sum(named * rank, axis=1, keepdims=True)
        place = jnp.where(live, dest.astype(F32) * 16.0 + nth * 4.0, -16.0)
        column = lax.broadcasted_iota(jnp.int32, (ROWS, N_PEER * 16), 1).astype(F32)
        for j in range(4):
            sel[j * ROWS:(j + 1) * ROWS, :] = jnp.where(column == place + float(j), 1.0, 0.0).astype(BF)
        for h in range(2):
            if h == 0:
                rcopy(a2a_recv.at[0], a2a_recv.at[0], a2a_ssem, a2a_rsem.at[0], partner).wait_recv()
            else:
                pltpu.make_async_copy(a2a_send.at[me], a2a_recv.at[1, me], own_sem).wait()
                rest = a2a_recv.at[1, pl.ds(0, N_PEER - 1)]
                rcopy(rest, rest, a2a_ssem, a2a_rsem.at[1], partner).wait_recv()
            for n in range(QUART // 128):
                block = a2a_recv[h, :, :, n * 128:(n + 1) * 128].reshape(N_PEER * 16, 128)
                picked = jnp.dot(sel[...], block, preferred_element_type=F32).astype(BF)
                for j in range(4):
                    lo = h * HALF + j * QUART + n * 128
                    cv[:, lo:lo + 128] = picked[j * ROWS:(j + 1) * ROWS, :]

    def out_at(t, k, a, b, c):
        if t == 0:
            cols = pl.ds(pl.multiple_of(a * ACOL + UP_OFF[k], 128), UP_W[k])
            return out_up.at[b, c, :, cols]
        return out_dn.at[a, b, c, pl.ds(DN_OFF[k], DN_H[k]), :]

    every = pl.ds(0, RING)
    lower, upper = pl.ds(0, 2), pl.ds(2, 2)

    def sems(t, k, i):
        return red_ssem.at[t, k, i], red_rsem.at[t, k, i]

    def ship(src, dst, t, k, i, device):
        rcopy(src, dst, *sems(t, k, i), device).start()

    def here(dst, t, k, i, device):
        wait_recv(dst, sems(t, k, i), device)

    def first_axis(k):
        return pos[ORDER[k][0]]

    def sides(k):
        axis = ORDER[k][0]
        return along(axis, -1), along(axis, 1)

    def stage1_send(t):
        for k in range(3):
            g, left, right = grad[t][k], *sides(k)
            ship(g.at[2, lower], rly[t][k].at[0], t, k, 0, right)
            ship(g.at[2, upper], rly[t][k].at[1], t, k, 1, left)
            ship(g.at[1, upper], inb[t][k].at[0, upper], t, k, 2, right)
            ship(g.at[3, lower], inb[t][k].at[1, lower], t, k, 3, left)

    def stage1_merge(t):
        for k in range(3):
            g, left, right = grad[t][k], *sides(k)
            here(rly[t][k].at[0], t, k, 0, left)
            g[1, 0:2] = (g[1, 0:2].astype(F32) + rly[t][k][0].astype(F32)).astype(BF)
            ship(g.at[1, lower], inb[t][k].at[0, lower], t, k, 4, right)
            here(rly[t][k].at[1], t, k, 1, right)
            g[3, 2:4] = (g[3, 2:4].astype(F32) + rly[t][k][1].astype(F32)).astype(BF)
            ship(g.at[3, upper], inb[t][k].at[1, upper], t, k, 5, left)

    def stage2_send(t):
        for k in range(3):
            g, left, right = grad[t][k], *sides(k)
            box, part = inb[t][k], s1[t][k]
            here(box.at[0, upper], t, k, 2, left)
            here(box.at[1, lower], t, k, 3, right)
            here(box.at[0, lower], t, k, 4, left)
            here(box.at[1, upper], t, k, 5, right)

            def add(b, carry, g=g, box=box, part=part):
                part[b] = (g[0, b].astype(F32) + box[0, b].astype(F32) + box[1, b].astype(F32)).astype(BF)
                return carry

            lax.fori_loop(0, RING, add, 0)
            axis = ORDER[k][1]
            for step in range(1, 4):
                ship(part.at[mod4(pos[axis] + step)], in2[t][k].at[step - 1], t, k, 5 + step, along(axis, step))

    def stage3_send(t):
        for k in range(3):
            axis = ORDER[k][1]
            box, part = in2[t][k], s2[t][k]
            for step in range(1, 4):
                here(box.at[step - 1], t, k, 5 + step, along(axis, -step))
            mine = s1[t][k][pos[axis]].astype(F32)
            part[...] = (mine + box[0].astype(F32) + box[1].astype(F32) + box[2].astype(F32)).astype(BF)
            axis = ORDER[k][2]
            for step in range(1, 4):
                ship(part.at[mod4(pos[axis] + step)], in3[t][k].at[step - 1], t, k, 8 + step, along(axis, step))

    def gather1_send(t):
        for k in range(3):
            a, b, c = (pos[axis] for axis in ORDER[k])
            axis = ORDER[k][2]
            box = in3[t][k]
            for step in range(1, 4):
                here(box.at[step - 1], t, k, 8 + step, along(axis, -step))
            mine = s2[t][k][c].astype(F32)
            whole = mine + box[0].astype(F32) + box[1].astype(F32) + box[2].astype(F32)
            piece = out_at(t, k, a, b, c)
            piece[...] = (whole * FACTOR).astype(BF)
            for step in range(1, 4):
                ship(piece, piece, t, k, 11 + step, along(axis, step))

    def gather2_send(t):
        for k in range(3):
            a, b, c = (pos[axis] for axis in ORDER[k])
            axis = ORDER[k][2]
            for step in range(1, 4):
                here(out_at(t, k, a, b, mod4(c - step)), t, k, 11 + step, along(axis, -step))
            axis = ORDER[k][1]
            line = out_at(t, k, a, b, every)
            for step in range(1, 4):
                ship(line, line, t, k, 14 + step, along(axis, step))

    def gather3_send(t):
        for k in range(3):
            a, b, c = (pos[axis] for axis in ORDER[k])
            axis = ORDER[k][1]
            for step in range(1, 4):
                here(out_at(t, k, a, mod4(b - step), every), t, k, 14 + step, along(axis, -step))
            left, right = sides(k)
            plane = out_at(t, k, a, every, every)
            ship(plane, plane, t, k, 18, right)
            ship(plane, plane, t, k, 19, left)

    def relay_send(t):
        for k in range(3):
            a = first_axis(k)
            left, right = sides(k)
            here(out_at(t, k, mod4(a - 1), every, every), t, k, 18, left)
            part = out_at(t, k, mod4(a - 1), lower, every)
            ship(part, part, t, k, 20, right)
            here(out_at(t, k, mod4(a + 1), every, every), t, k, 19, right)
            part = out_at(t, k, mod4(a + 1), upper, every)
            ship(part, part, t, k, 21, left)

    def finish(t):
        for k in range(3):
            a, b, c = (pos[axis] for axis in ORDER[k])
            left, right = sides(k)
            here(out_at(t, k, mod4(a + 2), lower, every), t, k, 20, left)
            here(out_at(t, k, mod4(a + 2), upper, every), t, k, 21, right)
            g = grad[t][k]

            def sent(src, i, t=t, k=k):
                wait_send(src, sems(t, k, i), partner)

            sent(g.at[2, lower], 0)
            sent(g.at[2, upper], 1)
            sent(g.at[1, upper], 2)
            sent(g.at[3, lower], 3)
            sent(g.at[1, lower], 4)
            sent(g.at[3, upper], 5)
            for step in range(1, 4):
                sent(s1[t][k].at[mod4(pos[ORDER[k][1]] + step)], 5 + step)
                sent(s2[t][k].at[mod4(pos[ORDER[k][2]] + step)], 8 + step)
                sent(out_at(t, k, a, b, c), 11 + step)
                sent(out_at(t, k, a, b, every), 14 + step)
            sent(out_at(t, k, a, every, every), 18)
            sent(out_at(t, k, a, every, every), 19)
            sent(out_at(t, k, mod4(a - 1), lower, every), 20)
            sent(out_at(t, k, mod4(a + 1), upper, every), 21)

    def make_up():
        def body(j, carry):
            for k in range(3):
                a = mod4(first_axis(k) + j)
                cols = pl.ds(pl.multiple_of(a * ACOL + UP_OFF[k], 128), UP_W[k])
                g = jnp.dot(act_t[...], cv[:, cols], preferred_element_type=F32)
                grad[0][k][j] = g.astype(BF).reshape(4, 4, 16, UP_W[k])
            return carry

        lax.fori_loop(0, RING, body, 0)
        stage1_send(0)

    def make_down(d_hidden):
        def body(j, carry):
            for k in range(3):
                a = mod4(first_axis(k) + j)
                h = DN_H[k]
                lhs = nt[a, :, DN_OFF[k]:DN_OFF[k] + h, :].reshape(16 * h, ROWS)
                g = jnp.dot(lhs, d_hidden, preferred_element_type=F32)
                grad[1][k][j] = g.astype(BF).reshape(4, 4, h, R)
            return carry

        lax.fori_loop(0, RING, body, 0)
        stage1_send(1)

    def hidden_grad(d_active):
        return (d_active * gate * (1.0 + hidden * (1.0 - gate))).astype(BF)

    def row_pass(d_hidden, send):
        mean = jnp.sum(d_hidden.astype(F32) * hidden, axis=1, keepdims=True) / D

        def body(c, carry):
            cols = cols_of(c)
            d_normed = lax.dot_general(d_hidden, wd_v[cols, :], INNER, preferred_element_type=F32)
            x_hat = x_v[:, cols].astype(F32) * inv
            gg[0, :, cols] = jnp.sum(d_normed * x_hat, axis=0, keepdims=True)
            d_in = cv[:, cols].astype(F32) + inv * (d_normed * gain_ref[:, cols] - x_hat * mean)
            out_rows[:, cols] = d_in.astype(BF)
            if send:
                rcopy(
                    out_rows.at[:, cols], cv.at[:, cols], row_ssem.at[c], row_rsem.at[c], partner
                ).start()
            return carry

        lax.fori_loop(0, N_CH, body, 0)

    @pl.when(sec == 1)
    def _():
        make_up()

        def body(c, acc):
            return acc + lax.dot_general(
                cv[:, cols_of(c)], wu_v[:, cols_of(c)], INNER, preferred_element_type=F32
            )

        d_hidden = hidden_grad(lax.fori_loop(0, N_CH, body, jnp.zeros((ROWS, R), F32)))
        row_pass(d_hidden, True)
        make_down(d_hidden)

    @pl.when(sec == 0)
    def _():
        def body(c, acc):
            row_wait(cv, c).wait_recv()
            return acc + lax.dot_general(
                cv[:, cols_of(c)], wu_v[:, cols_of(c)], INNER, preferred_element_type=F32
            )

        d_active = lax.fori_loop(0, N_CH, body, jnp.zeros((ROWS, R), F32))
        make_up()
        d_hidden = hidden_grad(d_active)
        make_down(d_hidden)
        row_pass(d_hidden, False)

    def gain_send(stage):
        axis = 2 - stage
        for step in range(1, 4):
            rcopy(
                gg.at[stage], gin.at[stage, step - 1],
                gain_ssem.at[stage, step - 1], gain_rsem.at[stage, step - 1], along(axis, step),
            ).start()

    def gain_add(stage):
        axis = 2 - stage
        for step in range(1, 4):
            wait_recv(
                gin.at[stage, step - 1],
                (gain_ssem.at[stage, step - 1], gain_rsem.at[stage, step - 1]), along(axis, -step),
            )
        gg[stage + 1] = gg[stage] + gin[stage, 0] + gin[stage, 1] + gin[stage, 2]

    gain_send(0)
    both = (0, 1)
    for t in both:
        stage1_merge(t)
    gain_add(0)
    gain_send(1)
    for t in both:
        stage2_send(t)
    gain_add(1)
    gain_send(2)
    for t in both:
        stage3_send(t)
    gain_add(2)
    out_gain[...] = (gg[3] * FACTOR).astype(BF)
    for t in both:
        gather1_send(t)
    for t in both:
        gather2_send(t)
    for t in both:
        gather3_send(t)
    for t in both:
        relay_send(t)
    for t in both:
        finish(t)

    for stage in range(3):
        for step in range(1, 4):
            wait_send(
                gg.at[stage], (gain_ssem.at[stage, step - 1], gain_rsem.at[stage, step - 1]), partner
            )

    @pl.when(sec == 0)
    def _():
        rcopy(a2a_send, a2a_send, a2a_ssem, a2a_rsem.at[0], partner).wait_send()

        def sent(c, carry):
            row_wait(fo, c).wait_send()
            return carry

        lax.fori_loop(0, N_CH, sent, 0)

    @pl.when(sec == 1)
    def _():
        rest = a2a_send.at[pl.ds(0, N_PEER - 1)]
        rcopy(rest, rest, a2a_ssem, a2a_rsem.at[1], partner).wait_send()

        def sent(c, carry):
            row_wait(out_rows, c).wait_send()
            return carry

        lax.fori_loop(0, N_CH, sent, 0)


def both_kinds(lead):
    ups = [pltpu.VMEM((*lead, 16, w), BF) for w in UP_W]
    downs = [pltpu.VMEM((*lead, h, R), BF) for h in DN_H]
    return ups + downs


def write_out(*refs):
    n = (len(refs) - 1) // 2
    sem = refs[-1]
    copies = [pltpu.make_async_copy(refs[i], refs[n + i], sem.at[i]) for i in range(n)]
    for copy in copies:
        copy.start()
    for copy in copies:
        copy.wait()


def shards(inputs, routes, counts, cotangent, gain_vector, w_down, w_up):
    hbm = pl.BlockSpec(memory_space=pl.ANY)
    vmem = pl.BlockSpec(memory_space=pltpu.VMEM)
    dma = pltpu.SemaphoreType.DMA
    scratch = [
        pltpu.VMEM((ROWS, D), BF),
        pltpu.VMEM((D, R), BF),
        pltpu.VMEM((R, D), BF),
        pltpu.VMEM((SLOTS, HALF), BF),
        pltpu.VMEM((N_PEER, 16, QUART), BF),
        pltpu.VMEM((2, N_PEER, 16, QUART), BF),
        pltpu.VMEM((RING, 16, 80, ROWS), BF),
        pltpu.VMEM((ROWS, D), BF),
        pltpu.VMEM((ROWS, D), BF),
        pltpu.VMEM((4 * ROWS, N_PEER * 16), BF),
        pltpu.VMEM((R, ROWS), BF),
    ]
    for lead in ((4, 4, 4), (2, 2, 4), (2, 4, 4), (4, 4), (3, 4), (4,), (3,)):
        scratch += both_kinds(lead)
    scratch += [
        pltpu.VMEM((4, 1, D), F32),
        pltpu.VMEM((3, 3, 1, D), F32),
        dma((4,)),
        dma,
        dma,
        dma((2,)),
        dma((N_CH,)),
        dma((N_CH,)),
        dma((2, 3, 22)),
        dma((2, 3, 22)),
        dma((3, 3)),
        dma((3, 3)),
    ]
    shapes = [(1, D), (RING, RING, RING, 80, R), (RING, RING, 16, D), (ROWS, D)]
    made = pl.pallas_call(
        kernel,
        out_shape=[pltpu.VMEM(s, BF) for s in shapes],
        in_specs=[hbm, vmem, vmem, hbm, vmem, hbm, hbm],
        out_specs=[vmem] * 4,
        scratch_shapes=scratch,
        compiler_params=pltpu.CompilerParams(
            collective_id=0, has_side_effects=True, vmem_limit_bytes=44 * 2**20
        ),
    )(inputs, routes, counts.reshape(1, 1), cotangent, gain_vector, w_down, w_up)
    gain, down, up, rows = pl.pallas_call(
        write_out,
        out_shape=[jax.ShapeDtypeStruct(s, BF) for s in shapes],
        in_specs=[vmem] * 4,
        out_specs=[hbm] * 4,
        scratch_shapes=[dma((4,))],
    )(*made)
    return gain, down.reshape(1, D, R), up.reshape(1, R, D), rows[None]


def solution(mesh):
    in_specs = (
        P("peer", None),
        P("peer", None),
        P("peer"),
        P("peer", None, None),
        P("section", None),
        P("section", None, None),
        P("section", None, None),
    )
    out_specs = (
        P("section", None),
        P("section", None, None),
        P("section", None, None),
        P("section", "peer", None),
    )
    return jax.shard_map(shards, mesh=mesh, in_specs=in_specs, out_specs=out_specs, check_vma=False)
```

```python
import jax
import jax.numpy as jnp
from jax import lax
from jax.experimental import pallas as pl
from jax.experimental.pallas import tpu as pltpu
from jax.sharding import PartitionSpec as P

rms_eps = 1e-05
MESH = pl.DeviceIdType.MESH
BF = jnp.bfloat16
F32 = jnp.float32

ROWS, D, R = 128, 5120, 256
SLOTS, CAP = 256, 4
N_PEER, RING = 64, 4
HALF = D // 2
QUART = HALF // 4
STRIDE, UNSTRIDE = 21, 3
GROUP = 16
N_GROUP = N_PEER // GROUP
CH = 640
N_CH = D // CH
ACOL = D // RING
UP_OFF, UP_W = (0, 384, 768), (384, 384, 512)
DN_OFF, DN_H = (0, 32, 64), (32, 32, 16)
ORDER = ((0, 1, 2), (1, 2, 0), (2, 0, 1))
FACTOR = float(N_PEER * ROWS) ** (-0.5)
INNER = (((1,), (1,)), ((), ()))


def mod4(v):
    return lax.rem(v + 8, 4)


def rcopy(src, dst, send_sem, recv_sem, device):
    return pltpu.make_async_remote_copy(
        src_ref=src,
        dst_ref=dst,
        send_sem=send_sem,
        recv_sem=recv_sem,
        device_id=device,
        device_id_type=MESH,
    )


def wait_recv(dst, sems, device):
    rcopy(dst, dst, sems[0], sems[1], device).wait_recv()


def wait_send(src, sems, device):
    rcopy(src, src, sems[0], sems[1], device).wait_send()


def kernel(
    x_hbm, routes_ref, counts_ref, cot_hbm, gain_hbm, wd_hbm, wu_hbm,
    out_gain, out_dn, out_up, out_rows,
    x_v, gain_ref, wd_v, wu_v, cot_v, a2a_send, a2a_recv, early_send, early_recv, nt, cv, fo, rest, sel, act_t,
    gu0, gu1, gu2, gd0, gd1, gd2,
    ru0, ru1, ru2, rd0, rd1, rd2,
    iu0, iu1, iu2, id0, id1, id2,
    su0, su1, su2, sd0, sd1, sd2,
    i2u0, i2u1, i2u2, i2d0, i2d1, i2d2,
    s2u0, s2u1, s2u2, s2d0, s2d1, s2d2,
    i3u0, i3u1, i3u2, i3d0, i3d1, i3d2,
    gg, gin,
    load_sem, own_sem, a2a_ssem, a2a_rsem, early_ssem, early_rsem, row_ssem, row_rsem, red_ssem, red_rsem, gain_ssem, gain_rsem,
):
    grad = ((gu0, gu1, gu2), (gd0, gd1, gd2))
    rly = ((ru0, ru1, ru2), (rd0, rd1, rd2))
    inb = ((iu0, iu1, iu2), (id0, id1, id2))
    s1 = ((su0, su1, su2), (sd0, sd1, sd2))
    in2 = ((i2u0, i2u1, i2u2), (i2d0, i2d1, i2d2))
    s2 = ((s2u0, s2u1, s2u2), (s2d0, s2d1, s2d2))
    in3 = ((i3u0, i3u1, i3u2), (i3d0, i3d1, i3d2))

    sec = lax.axis_index("section")
    me = lax.axis_index("peer")
    pos = (me // 16, lax.rem(me // 4, 4), lax.rem(me, 4))
    weight = (16, 4, 1)

    def along(axis, step):
        there = mod4(pos[axis] + step)
        return (sec, me + (there - pos[axis]) * weight[axis])

    partner = (1 - sec, me)

    def half_load(h):
        cols = pl.ds(h * HALF, HALF)
        return pltpu.make_async_copy(cot_hbm.at[0, :, cols], cot_v.at[:, cols], load_sem.at[h])

    wd_load = pltpu.make_async_copy(wd_hbm.at[0], wd_v, load_sem.at[2])
    wu_load = pltpu.make_async_copy(wu_hbm.at[0], wu_v, load_sem.at[3])
    x_load = pltpu.make_async_copy(x_hbm, x_v, load_sem.at[4])
    gain_load = pltpu.make_async_copy(gain_hbm, gain_ref, load_sem.at[5])
    half_load(0).start()

    @pl.when(sec == 0)
    def _():
        x_load.start()

    @pl.when(sec == 1)
    def _():
        half_load(1).start()

    wu_load.start()
    wd_load.start()
    gain_load.start()

    barrier = pltpu.get_barrier_semaphore()

    @pl.when(sec == 0)
    def _():
        pl.semaphore_signal(barrier, inc=1, device_id=partner, device_id_type=MESH)
        for axis in range(3):
            for step in range(1, 4):
                pl.semaphore_signal(barrier, inc=1, device_id=along(axis, step), device_id_type=MESH)

    @pl.when(sec == 1)
    def _():
        def greet(i, carry):
            pl.semaphore_signal(
                barrier, inc=1, device_id=(sec, lax.rem(me + i, N_PEER)), device_id_type=MESH
            )
            return carry

        lax.fori_loop(1, N_PEER, greet, 0)

    def cols_of(c):
        return pl.ds(pl.multiple_of(c * CH, CH), CH)

    half_load(0).wait()
    o_i = lax.broadcasted_iota(jnp.int32, (SLOTS, SLOTS), 0)
    i_i = lax.broadcasted_iota(jnp.int32, (SLOTS, SLOTS), 1)
    perm = jnp.where(i_i == (o_i & 3) * 64 + (o_i >> 2), 1.0, 0.0).astype(BF)

    def blocks(quarters, width):
        moved = jnp.dot(perm, jnp.concatenate(quarters, axis=0), preferred_element_type=F32)
        return moved.astype(BF).reshape(16, 16, width)

    def arrange(g, carry):
        rows = pl.ds(pl.multiple_of(g * 64, 64), 64)
        a2a_send[pl.ds(pl.multiple_of(g * 16, 16), 16)] = blocks(
            [cot_v[rows, pl.ds(pl.multiple_of(sec * HALF + j * QUART, 128), QUART)] for j in range(4)], QUART
        )
        return carry

    def peer_at(i):
        return lax.rem(me + i * STRIDE, N_PEER)

    def send_rows(h):
        def send(i, carry):
            dst = peer_at(i)
            rcopy(
                a2a_send.at[dst], a2a_recv.at[h, i], a2a_ssem, a2a_rsem.at[h, i // GROUP], (1, dst)
            ).start()
            return carry

        lax.fori_loop(h, N_PEER, send, 0)

    @pl.when(sec == 0)
    def _():
        lax.fori_loop(0, 4, arrange, 0)
        pl.semaphore_wait(barrier, 10)
        send_rows(0)

    @pl.when(sec == 1)
    def _():
        half_load(1).wait()
        wu_load.wait()

        def body(c, acc):
            return acc + lax.dot_general(
                cot_v[:, cols_of(c)], wu_v[:, cols_of(c)], INNER, preferred_element_type=F32
            )

        d_slot = lax.fori_loop(0, N_CH, body, jnp.zeros((SLOTS, R), F32))
        high = d_slot.astype(BF)
        low = (d_slot - high.astype(F32)).astype(BF)
        for g in range(4):
            rows = slice(g * 64, (g + 1) * 64)
            early_send[g * 16:(g + 1) * 16] = blocks(
                [part[rows, lo:lo + 128] for part in (high, low) for lo in (0, 128)], 128
            )
        pl.semaphore_wait(barrier, N_PEER)
        pl.semaphore_signal(barrier, inc=1, device_id=partner, device_id_type=MESH)
        pltpu.make_async_copy(early_send.at[me], early_recv.at[0], own_sem.at[0]).start()

        def send(i, carry):
            dst = peer_at(i)
            rcopy(early_send.at[dst], early_recv.at[i], early_ssem, early_rsem, (1, dst)).start()
            return carry

        lax.fori_loop(1, N_PEER, send, 0)
        lax.fori_loop(0, 4, arrange, 0)
        pltpu.make_async_copy(a2a_send.at[me], a2a_recv.at[1, 0], own_sem.at[1]).start()
        send_rows(1)

    def row_wait(ref, c):
        return rcopy(ref.at[:, cols_of(c)], ref.at[:, cols_of(c)], row_ssem.at[c], row_rsem.at[c], partner)

    @pl.when(sec == 0)
    def _():
        x_load.wait()

    def squares(c, total):
        @pl.when(sec == 1)
        def _():
            row_wait(x_v, c).wait_recv()

        xf = x_v[:, cols_of(c)].astype(F32)
        return total + jnp.sum(xf * xf, axis=1, keepdims=True)

    total = lax.fori_loop(0, N_CH, squares, jnp.zeros((ROWS, 1), F32))
    inv = lax.rsqrt(total / D + rms_eps)
    gain_load.wait()
    wd_load.wait()

    def down(c, hidden):
        xf = x_v[:, cols_of(c)].astype(F32)
        normed = (xf * inv * gain_ref[:, cols_of(c)]).astype(BF)
        nt[c // 2, pl.ds(pl.multiple_of(lax.rem(c, 2) * 8, 8), 8)] = normed.T.reshape(8, 80, ROWS)
        return hidden + jnp.dot(normed, wd_v[cols_of(c), :], preferred_element_type=F32)

    hidden = lax.fori_loop(0, N_CH, down, jnp.zeros((ROWS, R), F32))
    gate = jax.nn.sigmoid(hidden)
    active = (hidden * gate).astype(BF)
    act_t[...] = active.T
    @pl.when(sec == 0)
    def _():
        wu_load.wait()

        def up(c, carry):
            y = jnp.dot(active, wu_v[:, cols_of(c)], preferred_element_type=F32)
            fo[:, cols_of(c)] = (x_v[:, cols_of(c)].astype(F32) + y).astype(BF)
            rcopy(
                fo.at[:, cols_of(c)], x_v.at[:, cols_of(c)], row_ssem.at[c], row_rsem.at[c], partner
            ).start()
            return carry

        lax.fori_loop(0, N_CH, up, 0)

    def choose():
        dest = routes_ref[...]
        live = lax.broadcasted_iota(jnp.int32, (1, ROWS), 1) < counts_ref[...]
        lane = lax.broadcasted_iota(jnp.int32, (ROWS, ROWS), 1)
        row = lax.broadcasted_iota(jnp.int32, (ROWS, ROWS), 0)
        named = jnp.where((row == dest) & live, 1.0, 0.0)
        before = jnp.where(row < lane, 1.0, 0.0).astype(BF)
        rank = jnp.dot(named.astype(BF), before, preferred_element_type=F32)
        nth = jnp.sum(named * rank, axis=0, keepdims=True)
        turn = ((dest + (N_PEER - me)) * UNSTRIDE) & (N_PEER - 1)
        across = jnp.where(live, turn.astype(F32) * 16.0 + nth * 4.0, -16.0)
        place = jnp.sum(jnp.where(row == lane, across, 0.0), axis=1, keepdims=True)
        column = lax.broadcasted_iota(jnp.int32, (ROWS, N_PEER * 16), 1).astype(F32)
        for j in range(4):
            sel[j * ROWS:(j + 1) * ROWS, :] = jnp.where(column == place + float(j), 1.0, 0.0).astype(BF)

    def early_active():
        pltpu.make_async_copy(early_send.at[me], early_recv.at[0], own_sem.at[0]).wait()
        others = early_recv.at[pl.ds(1, N_PEER - 1)]
        rcopy(others, others, early_ssem, early_rsem, partner).wait_recv()
        got = jnp.dot(
            sel[...], early_recv[...].reshape(N_PEER * 16, 128), preferred_element_type=F32
        ).reshape(4, ROWS, 128)
        return jnp.concatenate([got[0] + got[2], got[1] + got[3]], axis=1)

    def pick(g):
        group = pl.ds(g * GROUP, GROUP)
        for h in range(2):
            landed = a2a_recv.at[h, group]
            if h == 1 and g == 0:
                pltpu.make_async_copy(a2a_send.at[me], a2a_recv.at[1, 0], own_sem.at[1]).wait()
                landed = a2a_recv.at[1, pl.ds(1, GROUP - 1)]
            rcopy(landed, landed, a2a_ssem, a2a_rsem.at[h, g], partner).wait_recv()
            picked = jnp.dot(
                sel[:, g * GROUP * 16:(g + 1) * GROUP * 16],
                a2a_recv[h, group].reshape(GROUP * 16, QUART),
                preferred_element_type=F32,
            ).astype(BF)
            for j in range(4):
                cols = pl.ds((h * 4 + j) * CH, CH)
                part = picked[j * ROWS:(j + 1) * ROWS, :]
                if g > 0:
                    part = cv[:, cols] + part
                cv[:, cols] = part
                if g == N_GROUP - 1:
                    out_rows[:, cols] = (part.astype(F32) + rest[:, cols]).astype(BF)
                    rcopy(
                        out_rows.at[:, cols], cv.at[:, cols],
                        row_ssem.at[h * 4 + j], row_rsem.at[h * 4 + j], partner,
                    ).start()

    def out_at(t, k, a, b, c):
        if t == 0:
            cols = pl.ds(pl.multiple_of(a * ACOL + UP_OFF[k], 128), UP_W[k])
            return out_up.at[b, c, :, cols]
        return out_dn.at[a, b, c, pl.ds(DN_OFF[k], DN_H[k]), :]

    every = pl.ds(0, RING)
    lower, upper = pl.ds(0, 2), pl.ds(2, 2)

    def sems(t, k, i):
        return red_ssem.at[t, k, i], red_rsem.at[t, k, i]

    def ship(src, dst, t, k, i, device):
        rcopy(src, dst, *sems(t, k, i), device).start()

    def here(dst, t, k, i, device):
        wait_recv(dst, sems(t, k, i), device)

    def first_axis(k):
        return pos[ORDER[k][0]]

    def sides(k):
        axis = ORDER[k][0]
        return along(axis, -1), along(axis, 1)

    def stage1_send(t):
        for k in range(3):
            g, left, right = grad[t][k], *sides(k)
            ship(g.at[2, lower], rly[t][k].at[0], t, k, 0, right)
            ship(g.at[2, upper], rly[t][k].at[1], t, k, 1, left)
            ship(g.at[1, upper], inb[t][k].at[0, upper], t, k, 2, right)
            ship(g.at[3, lower], inb[t][k].at[1, lower], t, k, 3, left)

    def stage1_merge(t):
        for k in range(3):
            g, left, right = grad[t][k], *sides(k)
            here(rly[t][k].at[0], t, k, 0, left)
            g[1, 0:2] = (g[1, 0:2].astype(F32) + rly[t][k][0].astype(F32)).astype(BF)
            ship(g.at[1, lower], inb[t][k].at[0, lower], t, k, 4, right)
            here(rly[t][k].at[1], t, k, 1, right)
            g[3, 2:4] = (g[3, 2:4].astype(F32) + rly[t][k][1].astype(F32)).astype(BF)
            ship(g.at[3, upper], inb[t][k].at[1, upper], t, k, 5, left)

    def stage2_send(t):
        for k in range(3):
            g, left, right = grad[t][k], *sides(k)
            box, part = inb[t][k], s1[t][k]
            here(box.at[0, upper], t, k, 2, left)
            here(box.at[1, lower], t, k, 3, right)
            here(box.at[0, lower], t, k, 4, left)
            here(box.at[1, upper], t, k, 5, right)

            def add(b, carry, g=g, box=box, part=part):
                part[b] = (g[0, b].astype(F32) + box[0, b].astype(F32) + box[1, b].astype(F32)).astype(BF)
                return carry

            lax.fori_loop(0, RING, add, 0)
            axis = ORDER[k][1]
            for step in range(1, 4):
                ship(part.at[mod4(pos[axis] + step)], in2[t][k].at[step - 1], t, k, 5 + step, along(axis, step))

    def stage3_send(t):
        for k in range(3):
            axis = ORDER[k][1]
            box, part = in2[t][k], s2[t][k]
            for step in range(1, 4):
                here(box.at[step - 1], t, k, 5 + step, along(axis, -step))
            mine = s1[t][k][pos[axis]].astype(F32)
            part[...] = (mine + box[0].astype(F32) + box[1].astype(F32) + box[2].astype(F32)).astype(BF)
            axis = ORDER[k][2]
            for step in range(1, 4):
                ship(part.at[mod4(pos[axis] + step)], in3[t][k].at[step - 1], t, k, 8 + step, along(axis, step))

    def gather1_send(t):
        for k in range(3):
            a, b, c = (pos[axis] for axis in ORDER[k])
            axis = ORDER[k][2]
            box = in3[t][k]
            for step in range(1, 4):
                here(box.at[step - 1], t, k, 8 + step, along(axis, -step))
            mine = s2[t][k][c].astype(F32)
            whole = mine + box[0].astype(F32) + box[1].astype(F32) + box[2].astype(F32)
            piece = out_at(t, k, a, b, c)
            piece[...] = (whole * FACTOR).astype(BF)
            for step in range(1, 4):
                ship(piece, piece, t, k, 11 + step, along(axis, step))

    def gather2_send(t):
        for k in range(3):
            a, b, c = (pos[axis] for axis in ORDER[k])
            axis = ORDER[k][2]
            for step in range(1, 4):
                here(out_at(t, k, a, b, mod4(c - step)), t, k, 11 + step, along(axis, -step))
            axis = ORDER[k][1]
            line = out_at(t, k, a, b, every)
            for step in range(1, 4):
                ship(line, line, t, k, 14 + step, along(axis, step))

    def gather3_send(t):
        for k in range(3):
            a, b, c = (pos[axis] for axis in ORDER[k])
            axis = ORDER[k][1]
            for step in range(1, 4):
                here(out_at(t, k, a, mod4(b - step), every), t, k, 14 + step, along(axis, -step))
            left, right = sides(k)
            low, high = out_at(t, k, a, lower, every), out_at(t, k, a, upper, every)
            ship(low, low, t, k, 18, right)
            ship(high, high, t, k, 19, left)
            ship(high, high, t, k, 20, right)
            ship(low, low, t, k, 21, left)

    def relay_send(t):
        for k in range(3):
            a = first_axis(k)
            left, right = sides(k)
            part = out_at(t, k, mod4(a - 1), lower, every)
            here(part, t, k, 18, left)
            ship(part, part, t, k, 22, right)
            part = out_at(t, k, mod4(a + 1), upper, every)
            here(part, t, k, 19, right)
            ship(part, part, t, k, 23, left)

    def finish(t):
        for k in range(3):
            a, b, c = (pos[axis] for axis in ORDER[k])
            left, right = sides(k)
            here(out_at(t, k, mod4(a - 1), upper, every), t, k, 20, left)
            here(out_at(t, k, mod4(a + 1), lower, every), t, k, 21, right)
            here(out_at(t, k, mod4(a + 2), lower, every), t, k, 22, left)
            here(out_at(t, k, mod4(a + 2), upper, every), t, k, 23, right)
            g = grad[t][k]

            def sent(src, i, t=t, k=k):
                wait_send(src, sems(t, k, i), partner)

            sent(g.at[2, lower], 0)
            sent(g.at[2, upper], 1)
            sent(g.at[1, upper], 2)
            sent(g.at[3, lower], 3)
            sent(g.at[1, lower], 4)
            sent(g.at[3, upper], 5)
            for step in range(1, 4):
                sent(s1[t][k].at[mod4(pos[ORDER[k][1]] + step)], 5 + step)
                sent(s2[t][k].at[mod4(pos[ORDER[k][2]] + step)], 8 + step)
                sent(out_at(t, k, a, b, c), 11 + step)
                sent(out_at(t, k, a, b, every), 14 + step)
            sent(out_at(t, k, a, lower, every), 18)
            sent(out_at(t, k, a, upper, every), 19)
            sent(out_at(t, k, a, upper, every), 20)
            sent(out_at(t, k, a, lower, every), 21)
            sent(out_at(t, k, mod4(a - 1), lower, every), 22)
            sent(out_at(t, k, mod4(a + 1), upper, every), 23)

    def make_up():
        def body(j, carry):
            for k in range(3):
                a = mod4(first_axis(k) + j)
                cols = pl.ds(pl.multiple_of(a * ACOL + UP_OFF[k], 128), UP_W[k])
                g = jnp.dot(act_t[...], cv[:, cols], preferred_element_type=F32)
                grad[0][k][j] = g.astype(BF).reshape(4, 4, 16, UP_W[k])
            return carry

        lax.fori_loop(0, RING, body, 0)
        stage1_send(0)

    def make_down(d_hidden):
        def body(j, carry):
            for k in range(3):
                a = mod4(first_axis(k) + j)
                h = DN_H[k]
                lhs = nt[a, :, DN_OFF[k]:DN_OFF[k] + h, :].reshape(16 * h, ROWS)
                g = jnp.dot(lhs, d_hidden, preferred_element_type=F32)
                grad[1][k][j] = g.astype(BF).reshape(4, 4, h, R)
            return carry

        lax.fori_loop(0, RING, body, 0)
        stage1_send(1)

    def hidden_grad(d_active):
        return (d_active * gate * (1.0 + hidden * (1.0 - gate))).astype(BF)

    def row_pass(d_hidden, last):
        mean = jnp.sum(d_hidden.astype(F32) * hidden, axis=1, keepdims=True) / D

        def body(c, carry):
            cols = cols_of(c)
            d_normed = lax.dot_general(d_hidden, wd_v[cols, :], INNER, preferred_element_type=F32)
            x_hat = x_v[:, cols].astype(F32) * inv
            gg[0, :, cols] = jnp.sum(d_normed * x_hat, axis=0, keepdims=True)
            change = inv * (d_normed * gain_ref[:, cols] - x_hat * mean)
            if last:
                out_rows[:, cols] = (cv[:, cols].astype(F32) + change).astype(BF)
            else:
                rest[:, cols] = change
            return carry

        lax.fori_loop(0, N_CH, body, 0)

    @pl.when(sec == 1)
    def _():
        choose()
        pick(0)
        d_hidden = hidden_grad(early_active())
        make_down(d_hidden)
        pick(1)
        row_pass(d_hidden, False)
        pick(2)
        pick(3)
        make_up()

    @pl.when(sec == 0)
    def _():
        def body(c, acc):
            row_wait(cv, c).wait_recv()
            return acc + lax.dot_general(
                cv[:, cols_of(c)], wu_v[:, cols_of(c)], INNER, preferred_element_type=F32
            )

        d_hidden = hidden_grad(lax.fori_loop(0, N_CH, body, jnp.zeros((ROWS, R), F32)))
        make_down(d_hidden)
        make_up()
        row_pass(d_hidden, True)

    def gain_send(stage):
        axis = 2 - stage
        for step in range(1, 4):
            rcopy(
                gg.at[stage], gin.at[stage, step - 1],
                gain_ssem.at[stage, step - 1], gain_rsem.at[stage, step - 1], along(axis, step),
            ).start()

    def gain_add(stage):
        axis = 2 - stage
        for step in range(1, 4):
            wait_recv(
                gin.at[stage, step - 1],
                (gain_ssem.at[stage, step - 1], gain_rsem.at[stage, step - 1]), along(axis, -step),
            )
        gg[stage + 1] = gg[stage] + gin[stage, 0] + gin[stage, 1] + gin[stage, 2]

    gain_send(0)
    both = (1, 0)
    for t in both:
        stage1_merge(t)
    gain_add(0)
    gain_send(1)
    for t in both:
        stage2_send(t)
    gain_add(1)
    gain_send(2)
    for t in both:
        stage3_send(t)
    gain_add(2)
    out_gain[...] = (gg[3] * FACTOR).astype(BF)
    for t in both:
        gather1_send(t)
    for t in both:
        gather2_send(t)
    for t in both:
        gather3_send(t)
    for t in both:
        relay_send(t)
    for t in both:
        finish(t)

    for stage in range(3):
        for step in range(1, 4):
            wait_send(
                gg.at[stage], (gain_ssem.at[stage, step - 1], gain_rsem.at[stage, step - 1]), partner
            )

    @pl.when(sec == 0)
    def _():
        rcopy(a2a_send, a2a_send, a2a_ssem, early_rsem, partner).wait_send()

        def sent(c, carry):
            row_wait(fo, c).wait_send()
            return carry

        lax.fori_loop(0, N_CH, sent, 0)

    @pl.when(sec == 1)
    def _():
        for sent_from, sem in ((a2a_send, a2a_ssem), (early_send, early_ssem)):
            others = sent_from.at[pl.ds(0, N_PEER - 1)]
            rcopy(others, others, sem, early_rsem, partner).wait_send()

        def sent(c, carry):
            row_wait(out_rows, c).wait_send()
            return carry

        lax.fori_loop(0, N_CH, sent, 0)


def both_kinds(lead):
    ups = [pltpu.VMEM((*lead, 16, w), BF) for w in UP_W]
    downs = [pltpu.VMEM((*lead, h, R), BF) for h in DN_H]
    return ups + downs


def write_out(*refs):
    n = (len(refs) - 1) // 2
    sem = refs[-1]
    copies = [pltpu.make_async_copy(refs[i], refs[n + i], sem.at[i]) for i in range(n)]
    for copy in copies:
        copy.start()
    for copy in copies:
        copy.wait()


def stay(operand):
    return pltpu.with_memory_space_constraint(operand, pltpu.HBM)


def shards(inputs, routes, counts, cotangent, gain_vector, w_down, w_up):
    hbm = pl.BlockSpec(memory_space=pltpu.HBM)
    vmem = pl.BlockSpec(memory_space=pltpu.VMEM)
    dma = pltpu.SemaphoreType.DMA
    scratch = [
        pltpu.VMEM((ROWS, D), BF),
        pltpu.VMEM((1, D), F32),
        pltpu.VMEM((D, R), BF),
        pltpu.VMEM((R, D), BF),
        pltpu.VMEM((SLOTS, D), BF),
        pltpu.VMEM((N_PEER, 16, QUART), BF),
        pltpu.VMEM((2, N_PEER, 16, QUART), BF),
        pltpu.VMEM((N_PEER, 16, 128), BF),
        pltpu.VMEM((N_PEER, 16, 128), BF),
        pltpu.VMEM((RING, 16, 80, ROWS), BF),
        pltpu.VMEM((ROWS, D), BF),
        pltpu.VMEM((ROWS, D), BF),
        pltpu.VMEM((ROWS, D), F32),
        pltpu.VMEM((4 * ROWS, N_PEER * 16), BF),
        pltpu.VMEM((R, ROWS), BF),
    ]
    for lead in ((4, 4, 4), (2, 2, 4), (2, 4, 4), (4, 4), (3, 4), (4,), (3,)):
        scratch += both_kinds(lead)
    scratch += [
        pltpu.VMEM((4, 1, D), F32),
        pltpu.VMEM((3, 3, 1, D), F32),
        dma((6,)),
        dma((2,)),
        dma,
        dma((2, N_GROUP)),
        dma,
        dma,
        dma((N_CH,)),
        dma((N_CH,)),
        dma((2, 3, 24)),
        dma((2, 3, 24)),
        dma((3, 3)),
        dma((3, 3)),
    ]
    shapes = [(1, D), (RING, RING, RING, 80, R), (RING, RING, 16, D), (ROWS, D)]
    made = pl.pallas_call(
        kernel,
        out_shape=[pltpu.VMEM(s, BF) for s in shapes],
        in_specs=[hbm, vmem, vmem, hbm, vmem, hbm, hbm],
        out_specs=[vmem] * 4,
        scratch_shapes=scratch,
        compiler_params=pltpu.CompilerParams(
            collective_id=0, has_side_effects=True, vmem_limit_bytes=44 * 2**20
        ),
    )(
        stay(inputs), routes.reshape(1, ROWS), counts.reshape(1, 1), stay(cotangent), stay(gain_vector),
        stay(w_down), stay(w_up),
    )
    gain, down, up, rows = pl.pallas_call(
        write_out,
        out_shape=[jax.ShapeDtypeStruct(s, BF) for s in shapes],
        in_specs=[vmem] * 4,
        out_specs=[hbm] * 4,
        scratch_shapes=[dma((4,))],
        compiler_params=pltpu.CompilerParams(vmem_limit_bytes=2**20),
    )(*made)
    return gain, down.reshape(1, D, R), up.reshape(1, R, D), rows[None]


def solution(mesh):
    in_specs = (
        P("peer", None),
        P("peer", None),
        P("peer"),
        P("peer", None, None),
        P("section", None),
        P("section", None, None),
        P("section", None, None),
    )
    out_specs = (
        P("section", None),
        P("section", None, None),
        P("section", None, None),
        P("section", "peer", None),
    )
    return jax.shard_map(shards, mesh=mesh, in_specs=in_specs, out_specs=out_specs, check_vma=False)
```

```python
import jax
import jax.numpy as jnp
from jax import lax
from jax.experimental import pallas as pl
from jax.experimental.pallas import tpu as pltpu
from jax.sharding import PartitionSpec as P

rms_eps = 1e-05
MESH = pl.DeviceIdType.MESH
BF = jnp.bfloat16
F32 = jnp.float32

ROWS, D, R = 128, 5120, 256
SLOTS, CAP = 256, 4
N_PEER, RING = 64, 4
HALF = D // 2
QUART = HALF // 4
GROUP = 16
N_GROUP = N_PEER // GROUP
UNROLL = 4
CH = 640
N_CH = D // CH
ACOL = D // RING
UP_OFF, UP_W = (0, 384, 768), (384, 384, 512)
DN_OFF, DN_H = (0, 32, 64), (32, 32, 16)
ORDER = ((0, 1, 2), (1, 2, 0), (2, 0, 1))
FACTOR = float(N_PEER * ROWS) ** (-0.5)
INNER = (((1,), (1,)), ((), ()))


def mod4(v):
    return lax.rem(v + 8, 4)


def rcopy(src, dst, send_sem, recv_sem, device):
    return pltpu.make_async_remote_copy(
        src_ref=src,
        dst_ref=dst,
        send_sem=send_sem,
        recv_sem=recv_sem,
        device_id=device,
        device_id_type=MESH,
    )


def wait_recv(dst, sems, device):
    rcopy(dst, dst, sems[0], sems[1], device).wait_recv()


def wait_send(src, sems, device):
    rcopy(src, src, sems[0], sems[1], device).wait_send()


def kernel(
    x_hbm, routes_hbm, counts_hbm, cot_hbm, gain_hbm, wd_hbm, wu_hbm,
    out_gain, out_dn, out_up, out_rows,
    x_v, routes_ref, counts_ref, gain_ref, wd_v, wu_v, cot_v, a2a_send, a2a_recv, early_send, early_recv, nt, cv, fo, rest, sel, act_t,
    gu0, gu1, gu2, gd0, gd1, gd2,
    ru0, ru1, ru2, rd0, rd1, rd2,
    iu0, iu1, iu2, id0, id1, id2,
    su0, su1, su2, sd0, sd1, sd2,
    i2u0, i2u1, i2u2, i2d0, i2d1, i2d2,
    i3u0, i3u1, i3u2, i3d0, i3d1, i3d2,
    gg, gin,
    load_sem, own_sem, a2a_ssem, a2a_rsem, early_ssem, early_rsem, row_ssem, row_rsem, red_ssem, red_rsem, gain_ssem, gain_rsem,
):
    grad = ((gu0, gu1, gu2), (gd0, gd1, gd2))
    rly = ((ru0, ru1, ru2), (rd0, rd1, rd2))
    inb = ((iu0, iu1, iu2), (id0, id1, id2))
    s1 = ((su0, su1, su2), (sd0, sd1, sd2))
    in2 = ((i2u0, i2u1, i2u2), (i2d0, i2d1, i2d2))
    in3 = ((i3u0, i3u1, i3u2), (i3d0, i3d1, i3d2))

    sec = lax.axis_index("section")
    me = lax.axis_index("peer")
    pos = (me // 16, lax.rem(me // 4, 4), lax.rem(me, 4))
    weight = (16, 4, 1)

    def along(axis, step):
        there = mod4(pos[axis] + step)
        return (sec, me + (there - pos[axis]) * weight[axis])

    partner = (1 - sec, me)

    def half_load(h):
        cols = pl.ds(h * HALF, HALF)
        return pltpu.make_async_copy(cot_hbm.at[0, :, cols], cot_v.at[:, cols], load_sem.at[h])

    wd_load = pltpu.make_async_copy(wd_hbm.at[0], wd_v, load_sem.at[2])
    wu_load = pltpu.make_async_copy(wu_hbm.at[0], wu_v, load_sem.at[3])
    x_load = pltpu.make_async_copy(x_hbm, x_v, load_sem.at[4])
    gain_load = pltpu.make_async_copy(gain_hbm, gain_ref, load_sem.at[5])
    routes_load = pltpu.make_async_copy(routes_hbm, routes_ref, load_sem.at[6])
    counts_load = pltpu.make_async_copy(counts_hbm, counts_ref, load_sem.at[7])
    barrier = pltpu.get_barrier_semaphore()

    def cols_of(c):
        return pl.ds(pl.multiple_of(c * CH, CH), CH)

    def blocks(quarters, width):
        o_i = lax.broadcasted_iota(jnp.int32, (SLOTS, SLOTS), 0)
        i_i = lax.broadcasted_iota(jnp.int32, (SLOTS, SLOTS), 1)
        perm = jnp.where(i_i == (o_i & 3) * 64 + (o_i >> 2), 1.0, 0.0).astype(BF)
        moved = jnp.dot(perm, jnp.concatenate(quarters, axis=0), preferred_element_type=F32)
        return moved.astype(BF).reshape(16, 16, width)

    def arrange(h):
        for g in range(4):
            rows = slice(g * 64, (g + 1) * 64)
            starts = [h * HALF + j * QUART for j in range(4)]
            a2a_send[g * 16:(g + 1) * 16] = blocks([cot_v[rows, lo:lo + QUART] for lo in starts], QUART)

    def peer_at(i):
        i2, i1, i0 = i // 16, lax.rem(i // 4, 4), lax.rem(i, 4)
        return mod4(pos[0] + i2 + i0) * 16 + mod4(pos[1] + i1 + i0) * 4 + mod4(pos[2] + i0)

    def send_rows(h):
        def send(i, carry):
            dst = peer_at(i)
            rcopy(
                a2a_send.at[dst], a2a_recv.at[h, i], a2a_ssem, a2a_rsem.at[h, i // GROUP], (1, dst)
            ).start()
            return carry

        lax.fori_loop(h, N_PEER, send, 0)

    def arrange_early():
        def body(c, acc):
            return acc + lax.dot_general(
                cot_v[:, cols_of(c)], wu_v[:, cols_of(c)], INNER, preferred_element_type=F32
            )

        d_slot = lax.fori_loop(0, N_CH, body, jnp.zeros((SLOTS, R), F32), unroll=UNROLL)
        high = d_slot.astype(BF)
        low = (d_slot - high.astype(F32)).astype(BF)
        for g in range(4):
            rows = slice(g * 64, (g + 1) * 64)
            early_send[g * 16:(g + 1) * 16] = blocks(
                [part[rows, lo:lo + 128] for part in (high, low) for lo in (0, 128)], 128
            )

    def send_early():
        pltpu.make_async_copy(early_send.at[me], early_recv.at[0], own_sem.at[0]).start()

        def send(i, carry):
            dst = peer_at(i)
            rcopy(early_send.at[dst], early_recv.at[i], early_ssem, early_rsem, (1, dst)).start()
            return carry

        lax.fori_loop(1, N_PEER, send, 0)

    def row_wait(ref, c):
        return rcopy(ref.at[:, cols_of(c)], ref.at[:, cols_of(c)], row_ssem.at[c], row_rsem.at[c], partner)

    def scaled(c):
        return (x_v[:, cols_of(c)].astype(F32) * gain_ref[:, cols_of(c)]).astype(BF)

    def turn_rows(c, carry):
        half = pl.ds(pl.multiple_of(lax.rem(c, 2) * 8, 8), 8)
        nt[c // 2, half] = scaled(c).T.reshape(8, 80, ROWS)
        return carry

    def forward(arriving):
        def down(c, carry):
            raw, total = carry
            if arriving:
                row_wait(x_v, c).wait_recv()
            xf = x_v[:, cols_of(c)].astype(F32)
            total = total + jnp.sum(xf * xf, axis=1, keepdims=True)
            return raw + jnp.dot(scaled(c), wd_v[cols_of(c), :], preferred_element_type=F32), total

        start = jnp.zeros((ROWS, R), F32), jnp.zeros((ROWS, 1), F32)
        raw, total = lax.fori_loop(0, N_CH, down, start, unroll=UNROLL)
        inv = lax.rsqrt(total / D + rms_eps)
        hidden = raw * inv
        gate = jax.nn.sigmoid(hidden)
        active = (hidden * gate).astype(BF)
        act_t[...] = active.T
        return inv, hidden, gate, active

    def choose():
        dest = routes_ref[...]
        live = lax.broadcasted_iota(jnp.int32, (1, ROWS), 1) < counts_ref[...]
        lane = lax.broadcasted_iota(jnp.int32, (ROWS, ROWS), 1)
        row = lax.broadcasted_iota(jnp.int32, (ROWS, ROWS), 0)
        named = jnp.where((row == dest) & live, 1.0, 0.0)
        before = jnp.where(row < lane, 1.0, 0.0).astype(BF)
        rank = jnp.dot(named.astype(BF), before, preferred_element_type=F32)
        nth = jnp.sum(named * rank, axis=0, keepdims=True)
        z = (pos[2] + 4 - (dest & 3)) & 3
        x = (pos[1] + 8 - ((dest >> 2) & 3) - z) & 3
        y = (pos[0] + 8 - (dest >> 4) - z) & 3
        turn = y * 16 + x * 4 + z
        across = jnp.where(live, turn.astype(F32) * 16.0 + nth * 4.0, -16.0)
        place = jnp.sum(jnp.where(row == lane, across, 0.0), axis=1, keepdims=True)
        column = lax.broadcasted_iota(jnp.int32, (ROWS, N_PEER * 16), 1).astype(F32)
        for j in range(4):
            sel[j * ROWS:(j + 1) * ROWS, :] = jnp.where(column == place + float(j), 1.0, 0.0).astype(BF)

    def early_active():
        pltpu.make_async_copy(early_send.at[me], early_recv.at[0], own_sem.at[0]).wait()
        others = early_recv.at[pl.ds(1, N_PEER - 1)]
        rcopy(others, others, early_ssem, early_rsem, partner).wait_recv()
        got = jnp.dot(
            sel[...], early_recv[...].reshape(N_PEER * 16, 128), preferred_element_type=F32
        ).reshape(4, ROWS, 128)
        return jnp.concatenate([got[0] + got[2], got[1] + got[3]], axis=1)

    def pick(g):
        group = pl.ds(g * GROUP, GROUP)
        for h in range(2):
            landed = a2a_recv.at[h, group]
            if h == 1 and g == 0:
                pltpu.make_async_copy(a2a_send.at[me], a2a_recv.at[1, 0], own_sem.at[1]).wait()
                landed = a2a_recv.at[1, pl.ds(1, GROUP - 1)]
            rcopy(landed, landed, a2a_ssem, a2a_rsem.at[h, g], partner).wait_recv()
            picked = jnp.dot(
                sel[:, g * GROUP * 16:(g + 1) * GROUP * 16],
                a2a_recv[h, group].reshape(GROUP * 16, QUART),
                preferred_element_type=F32,
            ).astype(BF)
            for j in range(4):
                cols = pl.ds((h * 4 + j) * CH, CH)
                part = picked[j * ROWS:(j + 1) * ROWS, :]
                if g > 0:
                    part = cv[:, cols] + part
                cv[:, cols] = part
                if g == N_GROUP - 1:
                    out_rows[:, cols] = (part.astype(F32) + rest[:, cols]).astype(BF)
                    rcopy(
                        out_rows.at[:, cols], cv.at[:, cols],
                        row_ssem.at[h * 4 + j], row_rsem.at[h * 4 + j], partner,
                    ).start()

    def out_at(t, k, a, b, c):
        if t == 0:
            cols = pl.ds(pl.multiple_of(a * ACOL + UP_OFF[k], 128), UP_W[k])
            return out_up.at[b, c, :, cols]
        return out_dn.at[a, b, c, pl.ds(DN_OFF[k], DN_H[k]), :]

    every = pl.ds(0, RING)
    lower, upper = pl.ds(0, 2), pl.ds(2, 2)

    def sems(t, k, i):
        return red_ssem.at[t, k], red_rsem.at[t, k, i]

    def ship(src, dst, t, k, i, device):
        rcopy(src, dst, *sems(t, k, i), device).start()

    def here(dst, t, k, i):
        wait_recv(dst, sems(t, k, i), partner)

    def first_axis(k):
        return pos[ORDER[k][0]]

    def sides(k):
        axis = ORDER[k][0]
        return along(axis, -1), along(axis, 1)

    def stage1_send(t):
        for k in range(3):
            g, left, right = grad[t][k], *sides(k)
            ship(g.at[2, lower], rly[t][k].at[0], t, k, 0, right)
            ship(g.at[2, upper], rly[t][k].at[1], t, k, 1, left)
            ship(g.at[1, upper], inb[t][k].at[0, upper], t, k, 2, right)
            ship(g.at[3, lower], inb[t][k].at[1, lower], t, k, 2, left)

    def stage1_merge(t):
        for k in range(3):
            g, left, right = grad[t][k], *sides(k)
            here(rly[t][k].at[0], t, k, 0)
            g[1, 0:2] = (g[1, 0:2].astype(F32) + rly[t][k][0].astype(F32)).astype(BF)
            ship(g.at[1, lower], inb[t][k].at[0, lower], t, k, 2, right)
            here(rly[t][k].at[1], t, k, 1)
            g[3, 2:4] = (g[3, 2:4].astype(F32) + rly[t][k][1].astype(F32)).astype(BF)
            ship(g.at[3, upper], inb[t][k].at[1, upper], t, k, 2, left)

    def stage2_send(t):
        for k in range(3):
            g, box, part = grad[t][k], inb[t][k], s1[t][k]
            here(box, t, k, 2)

            def add(b, carry, g=g, box=box, part=part):
                part[b] = (g[0, b].astype(F32) + box[0, b].astype(F32) + box[1, b].astype(F32)).astype(BF)
                return carry

            lax.fori_loop(0, RING, add, 0)
            axis = ORDER[k][1]
            for step in range(1, 4):
                ship(part.at[mod4(pos[axis] + step)], in2[t][k].at[step - 1], t, k, 3, along(axis, step))

    def stage3_send(t):
        for k in range(3):
            box, line = in2[t][k], in3[t][k]
            here(box, t, k, 3)
            mine = s1[t][k][pos[ORDER[k][1]]].astype(F32)
            axis = ORDER[k][2]
            part = line.at[pos[axis]]
            part[...] = (mine + box[0].astype(F32) + box[1].astype(F32) + box[2].astype(F32)).astype(BF)
            for step in range(1, 4):
                ship(part, part, t, k, 4, along(axis, step))

    def gather2_send(t):
        for k in range(3):
            a, b, _ = (pos[axis] for axis in ORDER[k])
            box = in3[t][k]
            here(box.at[0:3], t, k, 4)
            whole = box[0].astype(F32) + box[1].astype(F32) + box[2].astype(F32) + box[3].astype(F32)
            mine = out_at(t, k, a, b, every)
            mine[...] = (whole * FACTOR).astype(BF)
            axis = ORDER[k][1]
            for step in range(1, 4):
                ship(mine, mine, t, k, 6, along(axis, step))

    def gather3_send(t):
        for k in range(3):
            here(in2[t][k], t, k, 6)
            left, right = sides(k)
            a = first_axis(k)
            low, high = out_at(t, k, a, lower, every), out_at(t, k, a, upper, every)
            ship(low, low, t, k, 7, right)
            ship(high, high, t, k, 8, left)
            ship(high, high, t, k, 9, right)
            ship(low, low, t, k, 9, left)

    def relay_send(t):
        for k in range(3):
            a = first_axis(k)
            left, right = sides(k)
            part = out_at(t, k, mod4(a - 1), lower, every)
            here(part, t, k, 7)
            ship(part, part, t, k, 9, right)
            part = out_at(t, k, mod4(a + 1), upper, every)
            here(part, t, k, 8)
            ship(part, part, t, k, 9, left)

    def finish(t):
        for k in range(3):
            here(inb[t][k], t, k, 9)
            g = grad[t][k]
            for sent in (g, g, g.at[0, 0]):
                wait_send(sent, sems(t, k, 0), partner)

    def make_up():
        def body(j, carry):
            for k in range(3):
                a = mod4(first_axis(k) + j)
                cols = pl.ds(pl.multiple_of(a * ACOL + UP_OFF[k], 128), UP_W[k])
                g = jnp.dot(act_t[...], cv[:, cols], preferred_element_type=F32)
                grad[0][k][j] = g.astype(BF).reshape(4, 4, 16, UP_W[k])
            return carry

        lax.fori_loop(0, RING, body, 0)
        stage1_send(0)

    def make_down(d_hidden, inv):
        d_scaled = (d_hidden * inv).astype(BF)

        def body(j, carry):
            for k in range(3):
                a = mod4(first_axis(k) + j)
                h = DN_H[k]
                lhs = nt[a, :, DN_OFF[k]:DN_OFF[k] + h, :].reshape(16 * h, ROWS)
                g = jnp.dot(lhs, d_scaled, preferred_element_type=F32)
                grad[1][k][j] = g.astype(BF).reshape(4, 4, h, R)
            return carry

        lax.fori_loop(0, RING, body, 0)
        stage1_send(1)

    def hidden_grad(d_active, hidden, gate):
        return d_active * gate * (1.0 + hidden * (1.0 - gate))

    def row_pass(d_hidden, hidden, inv, last):
        d_hidden = d_hidden.astype(BF)
        mean = jnp.sum(d_hidden.astype(F32) * hidden, axis=1, keepdims=True) / D

        def body(c, carry):
            cols = cols_of(c)
            d_normed = lax.dot_general(d_hidden, wd_v[cols, :], INNER, preferred_element_type=F32)
            x_hat = x_v[:, cols].astype(F32) * inv
            gg[0, :, cols] = jnp.sum(d_normed * x_hat, axis=0, keepdims=True)
            change = inv * (d_normed * gain_ref[:, cols] - x_hat * mean)
            if last:
                out_rows[:, cols] = (cv[:, cols].astype(F32) + change).astype(BF)
            else:
                rest[:, cols] = change
            return carry

        lax.fori_loop(0, N_CH, body, 0, unroll=UNROLL)

    @pl.when(sec == 1)
    def _():
        half_load(1).start()
        half_load(0).start()
        wu_load.start()

        def greet(i, carry):
            pl.semaphore_signal(barrier, inc=1, device_id=(0, peer_at(i)), device_id_type=MESH)
            return carry

        lax.fori_loop(0, N_PEER, greet, 0)
        routes_load.start()
        counts_load.start()
        gain_load.start()
        wd_load.start()
        half_load(1).wait()
        arrange(1)
        half_load(0).wait()
        wu_load.wait()
        arrange_early()
        pl.semaphore_wait(barrier, 1)
        send_early()
        pltpu.make_async_copy(a2a_send.at[me], a2a_recv.at[1, 0], own_sem.at[1]).start()
        send_rows(1)
        routes_load.wait()
        counts_load.wait()
        choose()
        gain_load.wait()
        wd_load.wait()
        inv, hidden, gate, _ = forward(True)
        pick(0)
        lax.fori_loop(0, N_CH, turn_rows, 0, unroll=UNROLL)
        d_hidden = hidden_grad(early_active(), hidden, gate)
        make_down(d_hidden, inv)
        pick(1)
        row_pass(d_hidden, hidden, inv, False)
        pick(2)
        pick(3)
        make_up()

    @pl.when(sec == 0)
    def _():
        half_load(0).start()
        x_load.start()
        gain_load.start()
        wd_load.start()
        wu_load.start()
        for axis in range(3):
            for step in range(1, 4):
                pl.semaphore_signal(barrier, inc=1, device_id=along(axis, step), device_id_type=MESH)
        half_load(0).wait()
        arrange(0)
        pl.semaphore_wait(barrier, N_PEER + 9)
        pl.semaphore_signal(barrier, inc=1, device_id=partner, device_id_type=MESH)
        send_rows(0)
        x_load.wait()
        gain_load.wait()
        wd_load.wait()
        inv, hidden, gate, active = forward(False)
        wu_load.wait()

        def up(c, carry):
            y = jnp.dot(active, wu_v[:, cols_of(c)], preferred_element_type=F32)
            fo[:, cols_of(c)] = (x_v[:, cols_of(c)].astype(F32) + y).astype(BF)
            rcopy(
                fo.at[:, cols_of(c)], x_v.at[:, cols_of(c)], row_ssem.at[c], row_rsem.at[c], partner
            ).start()
            return carry

        lax.fori_loop(0, N_CH, up, 0, unroll=UNROLL)
        lax.fori_loop(0, N_CH, turn_rows, 0, unroll=UNROLL)

        def body(c, acc):
            row_wait(cv, c).wait_recv()
            return acc + lax.dot_general(
                cv[:, cols_of(c)], wu_v[:, cols_of(c)], INNER, preferred_element_type=F32
            )

        d_active = lax.fori_loop(0, N_CH, body, jnp.zeros((ROWS, R), F32), unroll=UNROLL)
        d_hidden = hidden_grad(d_active, hidden, gate)
        make_down(d_hidden, inv)
        make_up()
        row_pass(d_hidden, hidden, inv, True)

    def gain_send(stage):
        axis = 2 - stage
        for step in range(1, 4):
            rcopy(
                gg.at[stage], gin.at[stage, step - 1], gain_ssem, gain_rsem.at[stage], along(axis, step)
            ).start()

    def gain_add(stage):
        wait_recv(gin.at[stage], (gain_ssem, gain_rsem.at[stage]), partner)
        gg[stage + 1] = gg[stage] + gin[stage, 0] + gin[stage, 1] + gin[stage, 2]

    gain_send(0)
    both = (1, 0)
    for t in both:
        stage1_merge(t)
    gain_add(0)
    gain_send(1)
    for t in both:
        stage2_send(t)
    gain_add(1)
    gain_send(2)
    for t in both:
        stage3_send(t)
    gain_add(2)
    out_gain[...] = (gg[3] * FACTOR).astype(BF)
    for t in both:
        gather2_send(t)
    for t in both:
        gather3_send(t)
    for t in both:
        relay_send(t)
    for t in both:
        finish(t)

    wait_send(gin, (gain_ssem, gain_rsem.at[0]), partner)

    @pl.when(sec == 0)
    def _():
        rcopy(a2a_send, a2a_send, a2a_ssem, early_rsem, partner).wait_send()

        def sent(c, carry):
            row_wait(fo, c).wait_send()
            return carry

        lax.fori_loop(0, N_CH, sent, 0)

    @pl.when(sec == 1)
    def _():
        for sent_from, sem in ((a2a_send, a2a_ssem), (early_send, early_ssem)):
            others = sent_from.at[pl.ds(0, N_PEER - 1)]
            rcopy(others, others, sem, early_rsem, partner).wait_send()

        def sent(c, carry):
            row_wait(out_rows, c).wait_send()
            return carry

        lax.fori_loop(0, N_CH, sent, 0)


def both_kinds(lead):
    ups = [pltpu.VMEM((*lead, 16, w), BF) for w in UP_W]
    downs = [pltpu.VMEM((*lead, h, R), BF) for h in DN_H]
    return ups + downs


def write_out(*refs):
    n = (len(refs) - 1) // 2
    sem = refs[-1]
    copies = [pltpu.make_async_copy(refs[i], refs[n + i], sem.at[i]) for i in range(n)]
    for copy in copies:
        copy.start()
    for copy in copies:
        copy.wait()


def stay(operand):
    return pltpu.with_memory_space_constraint(operand, pltpu.HBM)


def shards(inputs, routes, counts, cotangent, gain_vector, w_down, w_up):
    hbm = pl.BlockSpec(memory_space=pltpu.HBM)
    vmem = pl.BlockSpec(memory_space=pltpu.VMEM)
    anywhere = pl.BlockSpec(memory_space=pl.ANY)
    dma = pltpu.SemaphoreType.DMA
    scratch = [
        pltpu.VMEM((ROWS, D), BF),
        pltpu.VMEM((1, ROWS), jnp.int32),
        pltpu.VMEM((1, 1), jnp.int32),
        pltpu.VMEM((1, D), F32),
        pltpu.VMEM((D, R), BF),
        pltpu.VMEM((R, D), BF),
        pltpu.VMEM((SLOTS, D), BF),
        pltpu.VMEM((N_PEER, 16, QUART), BF),
        pltpu.VMEM((2, N_PEER, 16, QUART), BF),
        pltpu.VMEM((N_PEER, 16, 128), BF),
        pltpu.VMEM((N_PEER, 16, 128), BF),
        pltpu.VMEM((RING, 16, 80, ROWS), BF),
        pltpu.VMEM((ROWS, D), BF),
        pltpu.VMEM((ROWS, D), BF),
        pltpu.VMEM((ROWS, D), F32),
        pltpu.VMEM((4 * ROWS, N_PEER * 16), BF),
        pltpu.VMEM((R, ROWS), BF),
    ]
    for lead in ((4, 4, 4), (2, 2, 4), (2, 4, 4), (4, 4), (3, 4), (4, 4)):
        scratch += both_kinds(lead)
    scratch += [
        pltpu.VMEM((4, 1, D), F32),
        pltpu.VMEM((3, 3, 1, D), F32),
        dma((8,)),
        dma((2,)),
        dma,
        dma((2, N_GROUP)),
        dma,
        dma,
        dma((N_CH,)),
        dma((N_CH,)),
        dma((2, 3)),
        dma((2, 3, 10)),
        dma,
        dma((3,)),
    ]
    shapes = [(1, D), (RING, RING, RING, 80, R), (RING, RING, 16, D), (ROWS, D)]
    made = pl.pallas_call(
        kernel,
        out_shape=[pltpu.VMEM(s, BF) for s in shapes],
        in_specs=[hbm, anywhere, anywhere, hbm, hbm, hbm, hbm],
        out_specs=[vmem] * 4,
        scratch_shapes=scratch,
        compiler_params=pltpu.CompilerParams(
            collective_id=0, has_side_effects=True, vmem_limit_bytes=44 * 2**20
        ),
    )(
        stay(inputs), routes.reshape(1, ROWS), counts.reshape(1, 1), stay(cotangent), stay(gain_vector),
        stay(w_down), stay(w_up),
    )
    gain, down, up, rows = pl.pallas_call(
        write_out,
        out_shape=[jax.ShapeDtypeStruct(s, BF) for s in shapes],
        in_specs=[vmem] * 4,
        out_specs=[hbm] * 4,
        scratch_shapes=[dma((4,))],
        compiler_params=pltpu.CompilerParams(vmem_limit_bytes=2**20),
    )(*made)
    return gain, down.reshape(1, D, R), up.reshape(1, R, D), rows[None]


def solution(mesh):
    in_specs = (
        P("peer", None),
        P("peer", None),
        P("peer"),
        P("peer", None, None),
        P("section", None),
        P("section", None, None),
        P("section", None, None),
    )
    out_specs = (
        P("section", None),
        P("section", None, None),
        P("section", None, None),
        P("section", "peer", None),
    )
    return jax.shard_map(shards, mesh=mesh, in_specs=in_specs, out_specs=out_specs, check_vma=False)
```

```python
import jax
import jax.numpy as jnp
from jax import lax
from jax.experimental import pallas as pl
from jax.experimental.pallas import tpu as pltpu
from jax.sharding import PartitionSpec as P

rms_eps = 1e-05
MESH = pl.DeviceIdType.MESH
BF = jnp.bfloat16
F32 = jnp.float32

ROWS, D, R = 128, 5120, 256
SLOTS, CAP = 256, 4
N_PEER, RING = 64, 4
HALF = D // 2
QUART = HALF // 4
GROUP = 16
N_GROUP = N_PEER // GROUP
UNROLL = 4
CH = 640
N_CH = D // CH
ACOL = D // RING
UP_OFF, UP_W = (0, 384, 768), (384, 384, 512)
DN_OFF, DN_H = (0, 32, 64), (32, 32, 16)
ORDER = ((0, 1, 2), (1, 2, 0), (2, 0, 1))
FACTOR = float(N_PEER * ROWS) ** (-0.5)
INNER = (((1,), (1,)), ((), ()))


def mod4(v):
    return lax.rem(v + 8, 4)


def rcopy(src, dst, send_sem, recv_sem, device):
    return pltpu.make_async_remote_copy(
        src_ref=src,
        dst_ref=dst,
        send_sem=send_sem,
        recv_sem=recv_sem,
        device_id=device,
        device_id_type=MESH,
    )


def wait_recv(dst, sems, device):
    rcopy(dst, dst, sems[0], sems[1], device).wait_recv()


def wait_send(src, sems, device):
    rcopy(src, src, sems[0], sems[1], device).wait_send()


def kernel(
    x_hbm, routes_hbm, counts_hbm, cot_hbm, gain_hbm, wd_hbm, wu_hbm,
    out_gain, out_dn, out_up, out_rows,
    x_v, routes_ref, counts_ref, gain_ref, wd_v, wu_v, cot_v, a2a_send, a2a_recv, early_send, early_recv, nt, cv, fo, rest, sel, act_t,
    gu0, gu1, gu2, gd0, gd1, gd2,
    ru0, ru1, ru2, rd0, rd1, rd2,
    iu0, iu1, iu2, id0, id1, id2,
    su0, su1, su2, sd0, sd1, sd2,
    i2u0, i2u1, i2u2, i2d0, i2d1, i2d2,
    i3u0, i3u1, i3u2, i3d0, i3d1, i3d2,
    gg, gin,
    load_sem, own_sem, a2a_ssem, a2a_rsem, early_ssem, early_rsem, row_ssem, row_rsem, red_ssem, red_rsem, gain_ssem, gain_rsem,
):
    grad = ((gu0, gu1, gu2), (gd0, gd1, gd2))
    rly = ((ru0, ru1, ru2), (rd0, rd1, rd2))
    inb = ((iu0, iu1, iu2), (id0, id1, id2))
    s1 = ((su0, su1, su2), (sd0, sd1, sd2))
    in2 = ((i2u0, i2u1, i2u2), (i2d0, i2d1, i2d2))
    in3 = ((i3u0, i3u1, i3u2), (i3d0, i3d1, i3d2))

    sec = lax.axis_index("section")
    me = lax.axis_index("peer")
    pos = (me // 16, lax.rem(me // 4, 4), lax.rem(me, 4))
    weight = (16, 4, 1)

    def along(axis, step):
        there = mod4(pos[axis] + step)
        return (sec, me + (there - pos[axis]) * weight[axis])

    partner = (1 - sec, me)

    def half_load(h):
        cols = pl.ds(h * HALF, HALF)
        return pltpu.make_async_copy(cot_hbm.at[0, :, cols], cot_v.at[:, cols], load_sem.at[h])

    wd_load = pltpu.make_async_copy(wd_hbm.at[0], wd_v, load_sem.at[2])
    wu_load = pltpu.make_async_copy(wu_hbm.at[0], wu_v, load_sem.at[3])
    x_load = pltpu.make_async_copy(x_hbm, x_v, load_sem.at[4])
    gain_load = pltpu.make_async_copy(gain_hbm, gain_ref, load_sem.at[5])
    routes_load = pltpu.make_async_copy(routes_hbm, routes_ref, load_sem.at[6])
    counts_load = pltpu.make_async_copy(counts_hbm, counts_ref, load_sem.at[7])
    barrier = pltpu.get_barrier_semaphore()

    def cols_of(c):
        return pl.ds(pl.multiple_of(c * CH, CH), CH)

    def blocks(quarters, width):
        o_i = lax.broadcasted_iota(jnp.int32, (SLOTS, SLOTS), 0)
        i_i = lax.broadcasted_iota(jnp.int32, (SLOTS, SLOTS), 1)
        perm = jnp.where(i_i == (o_i & 3) * 64 + (o_i >> 2), 1.0, 0.0).astype(BF)
        moved = jnp.dot(perm, jnp.concatenate(quarters, axis=0), preferred_element_type=F32)
        return moved.astype(BF).reshape(16, 16, width)

    def arrange(h):
        for g in range(4):
            rows = slice(g * 64, (g + 1) * 64)
            starts = [h * HALF + j * QUART for j in range(4)]
            a2a_send[g * 16:(g + 1) * 16] = blocks([cot_v[rows, lo:lo + QUART] for lo in starts], QUART)

    def peer_at(i):
        i2, i1, i0 = i // 16, lax.rem(i // 4, 4), lax.rem(i, 4)
        return mod4(pos[0] + i2 + i0) * 16 + mod4(pos[1] + i1 + i0) * 4 + mod4(pos[2] + i0)

    def send_rows(h):
        def send(i, carry):
            dst = peer_at(i)
            rcopy(
                a2a_send.at[dst], a2a_recv.at[h, i], a2a_ssem, a2a_rsem.at[h, i // GROUP], (1, dst)
            ).start()
            return carry

        lax.fori_loop(h, N_PEER, send, 0)

    def arrange_early():
        def body(c, acc):
            return acc + lax.dot_general(
                cot_v[:, cols_of(c)], wu_v[:, cols_of(c)], INNER, preferred_element_type=F32
            )

        d_slot = lax.fori_loop(0, N_CH, body, jnp.zeros((SLOTS, R), F32), unroll=UNROLL)
        high = d_slot.astype(BF)
        low = (d_slot - high.astype(F32)).astype(BF)
        for g in range(4):
            rows = slice(g * 64, (g + 1) * 64)
            early_send[g * 16:(g + 1) * 16] = blocks(
                [part[rows, lo:lo + 128] for part in (high, low) for lo in (0, 128)], 128
            )

    def send_early():
        pltpu.make_async_copy(early_send.at[me], early_recv.at[0], own_sem.at[0]).start()

        def send(i, carry):
            dst = peer_at(i)
            rcopy(early_send.at[dst], early_recv.at[i], early_ssem, early_rsem, (1, dst)).start()
            return carry

        lax.fori_loop(1, N_PEER, send, 0)

    def row_wait(ref, c):
        return rcopy(ref.at[:, cols_of(c)], ref.at[:, cols_of(c)], row_ssem.at[c], row_rsem.at[c], partner)

    def scaled(c):
        return (x_v[:, cols_of(c)].astype(F32) * gain_ref[:, cols_of(c)]).astype(BF)

    def turn_rows(c, carry):
        half = pl.ds(pl.multiple_of(lax.rem(c, 2) * 8, 8), 8)
        nt[c // 2, half] = scaled(c).T.reshape(8, 80, ROWS)
        return carry

    def forward(arriving):
        def down(c, carry):
            raw, total = carry
            if arriving:
                row_wait(x_v, c).wait_recv()
            xf = x_v[:, cols_of(c)].astype(F32)
            total = total + jnp.sum(xf * xf, axis=1, keepdims=True)
            return raw + jnp.dot(scaled(c), wd_v[cols_of(c), :], preferred_element_type=F32), total

        start = jnp.zeros((ROWS, R), F32), jnp.zeros((ROWS, 1), F32)
        raw, total = lax.fori_loop(0, N_CH, down, start, unroll=UNROLL)
        inv = lax.rsqrt(total / D + rms_eps)
        hidden = raw * inv
        gate = jax.nn.sigmoid(hidden)
        active = (hidden * gate).astype(BF)
        act_t[...] = active.T
        return inv, hidden, gate, active

    def choose():
        dest = routes_ref[...]
        live = lax.broadcasted_iota(jnp.int32, (1, ROWS), 1) < counts_ref[...]
        lane = lax.broadcasted_iota(jnp.int32, (ROWS, ROWS), 1)
        row = lax.broadcasted_iota(jnp.int32, (ROWS, ROWS), 0)
        named = jnp.where((row == dest) & live, 1.0, 0.0)
        before = jnp.where(row < lane, 1.0, 0.0).astype(BF)
        rank = jnp.dot(named.astype(BF), before, preferred_element_type=F32)
        nth = jnp.sum(named * rank, axis=0, keepdims=True)
        z = (pos[2] + 4 - (dest & 3)) & 3
        x = (pos[1] + 8 - ((dest >> 2) & 3) - z) & 3
        y = (pos[0] + 8 - (dest >> 4) - z) & 3
        turn = y * 16 + x * 4 + z
        across = jnp.where(live, turn.astype(F32) * 16.0 + nth * 4.0, -16.0)
        place = jnp.sum(jnp.where(row == lane, across, 0.0), axis=1, keepdims=True)
        column = lax.broadcasted_iota(jnp.int32, (ROWS, N_PEER * 16), 1).astype(F32)
        for j in range(4):
            sel[j * ROWS:(j + 1) * ROWS, :] = jnp.where(column == place + float(j), 1.0, 0.0).astype(BF)

    def early_active():
        pltpu.make_async_copy(early_send.at[me], early_recv.at[0], own_sem.at[0]).wait()
        others = early_recv.at[pl.ds(1, N_PEER - 1)]
        rcopy(others, others, early_ssem, early_rsem, partner).wait_recv()
        got = jnp.dot(
            sel[...], early_recv[...].reshape(N_PEER * 16, 128), preferred_element_type=F32
        ).reshape(4, ROWS, 128)
        return jnp.concatenate([got[0] + got[2], got[1] + got[3]], axis=1)

    def pick(g):
        group = pl.ds(g * GROUP, GROUP)
        for h in range(2):
            landed = a2a_recv.at[h, group]
            if h == 1 and g == 0:
                pltpu.make_async_copy(a2a_send.at[me], a2a_recv.at[1, 0], own_sem.at[1]).wait()
                landed = a2a_recv.at[1, pl.ds(1, GROUP - 1)]
            rcopy(landed, landed, a2a_ssem, a2a_rsem.at[h, g], partner).wait_recv()
            picked = jnp.dot(
                sel[:, g * GROUP * 16:(g + 1) * GROUP * 16],
                a2a_recv[h, group].reshape(GROUP * 16, QUART),
                preferred_element_type=F32,
            ).astype(BF)
            for j in range(4):
                cols = pl.ds((h * 4 + j) * CH, CH)
                part = picked[j * ROWS:(j + 1) * ROWS, :]
                if g > 0:
                    part = cv[:, cols] + part
                cv[:, cols] = part
                if g == N_GROUP - 1:
                    out_rows[:, cols] = (part.astype(F32) + rest[:, cols]).astype(BF)
                    rcopy(
                        out_rows.at[:, cols], cv.at[:, cols],
                        row_ssem.at[h * 4 + j], row_rsem.at[h * 4 + j], partner,
                    ).start()

    def out_at(t, k, a, b, c):
        if t == 0:
            cols = pl.ds(pl.multiple_of(a * ACOL + UP_OFF[k], 128), UP_W[k])
            return out_up.at[b, c, :, cols]
        return out_dn.at[a, b, c, pl.ds(DN_OFF[k], DN_H[k]), :]

    every = pl.ds(0, RING)
    lower, upper = pl.ds(0, 2), pl.ds(2, 2)

    def sems(t, k, i):
        return red_ssem.at[t, k], red_rsem.at[t, k, i]

    def ship(src, dst, t, k, i, device):
        rcopy(src, dst, *sems(t, k, i), device).start()

    def here(dst, t, k, i):
        wait_recv(dst, sems(t, k, i), partner)

    def first_axis(k):
        return pos[ORDER[k][0]]

    def sides(k):
        axis = ORDER[k][0]
        return along(axis, -1), along(axis, 1)

    def stage1_send(t):
        for k in range(3):
            g, left, right = grad[t][k], *sides(k)
            ship(g.at[2, lower], rly[t][k].at[0], t, k, 0, right)
            ship(g.at[2, upper], rly[t][k].at[1], t, k, 1, left)
            ship(g.at[1, upper], inb[t][k].at[0, upper], t, k, 2, right)
            ship(g.at[3, lower], inb[t][k].at[1, lower], t, k, 2, left)

    def stage1_merge(t):
        for k in range(3):
            g, left, right = grad[t][k], *sides(k)
            here(rly[t][k].at[0], t, k, 0)
            g[1, 0:2] = (g[1, 0:2].astype(F32) + rly[t][k][0].astype(F32)).astype(BF)
            ship(g.at[1, lower], inb[t][k].at[0, lower], t, k, 2, right)
            here(rly[t][k].at[1], t, k, 1)
            g[3, 2:4] = (g[3, 2:4].astype(F32) + rly[t][k][1].astype(F32)).astype(BF)
            ship(g.at[3, upper], inb[t][k].at[1, upper], t, k, 2, left)

    def stage2_send(t):
        for k in range(3):
            g, box, part = grad[t][k], inb[t][k], s1[t][k]
            here(box, t, k, 2)

            def add(b, carry, g=g, box=box, part=part):
                part[b] = (g[0, b].astype(F32) + box[0, b].astype(F32) + box[1, b].astype(F32)).astype(BF)
                return carry

            lax.fori_loop(0, RING, add, 0)
            axis = ORDER[k][1]
            for step in range(1, 4):
                ship(part.at[mod4(pos[axis] + step)], in2[t][k].at[step - 1], t, k, 3, along(axis, step))

    def stage3_send(t):
        for k in range(3):
            box, line = in2[t][k], in3[t][k]
            here(box, t, k, 3)
            mine = s1[t][k][pos[ORDER[k][1]]].astype(F32)
            axis = ORDER[k][2]
            part = line.at[pos[axis]]
            part[...] = (mine + box[0].astype(F32) + box[1].astype(F32) + box[2].astype(F32)).astype(BF)
            for step in range(1, 4):
                ship(part, part, t, k, 4, along(axis, step))

    def gather2_send(t):
        for k in range(3):
            a, b, _ = (pos[axis] for axis in ORDER[k])
            box = in3[t][k]
            here(box.at[0:3], t, k, 4)
            whole = box[0].astype(F32) + box[1].astype(F32) + box[2].astype(F32) + box[3].astype(F32)
            mine = out_at(t, k, a, b, every)
            mine[...] = (whole * FACTOR).astype(BF)
            axis = ORDER[k][1]
            for step in range(1, 4):
                ship(mine, mine, t, k, 6, along(axis, step))

    def gather3_send(t):
        for k in range(3):
            here(in2[t][k], t, k, 6)
            left, right = sides(k)
            a = first_axis(k)
            low, high = out_at(t, k, a, lower, every), out_at(t, k, a, upper, every)
            ship(low, low, t, k, 7, right)
            ship(high, high, t, k, 8, left)
            ship(high, high, t, k, 9, right)
            ship(low, low, t, k, 9, left)

    def relay_send(t):
        for k in range(3):
            a = first_axis(k)
            left, right = sides(k)
            part = out_at(t, k, mod4(a - 1), lower, every)
            here(part, t, k, 7)
            ship(part, part, t, k, 9, right)
            part = out_at(t, k, mod4(a + 1), upper, every)
            here(part, t, k, 8)
            ship(part, part, t, k, 9, left)

    def finish(t):
        for k in range(3):
            here(inb[t][k], t, k, 9)
            g = grad[t][k]
            for sent in (g, g, g.at[0, 0]):
                wait_send(sent, sems(t, k, 0), partner)

    def make_up():
        def body(j, carry):
            for k in range(3):
                a = mod4(first_axis(k) + j)
                cols = pl.ds(pl.multiple_of(a * ACOL + UP_OFF[k], 128), UP_W[k])
                g = jnp.dot(act_t[...], cv[:, cols], preferred_element_type=F32)
                grad[0][k][j] = g.astype(BF).reshape(4, 4, 16, UP_W[k])
            return carry

        lax.fori_loop(0, RING, body, 0, unroll=UNROLL)
        stage1_send(0)

    def make_down(d_hidden, inv):
        d_scaled = (d_hidden * inv).astype(BF)

        def body(j, carry):
            for k in range(3):
                a = mod4(first_axis(k) + j)
                h = DN_H[k]
                lhs = nt[a, :, DN_OFF[k]:DN_OFF[k] + h, :].reshape(16 * h, ROWS)
                g = jnp.dot(lhs, d_scaled, preferred_element_type=F32)
                grad[1][k][j] = g.astype(BF).reshape(4, 4, h, R)
            return carry

        lax.fori_loop(0, RING, body, 0, unroll=UNROLL)
        stage1_send(1)

    def hidden_grad(d_active, hidden, gate):
        return d_active * gate * (1.0 + hidden * (1.0 - gate))

    def row_pass(d_hidden, hidden, inv, last):
        d_hidden = d_hidden.astype(BF)
        mean = jnp.sum(d_hidden.astype(F32) * hidden, axis=1, keepdims=True) / D

        def body(c, carry):
            cols = cols_of(c)
            d_normed = lax.dot_general(d_hidden, wd_v[cols, :], INNER, preferred_element_type=F32)
            x_hat = x_v[:, cols].astype(F32) * inv
            gg[0, :, cols] = jnp.sum(d_normed * x_hat, axis=0, keepdims=True)
            change = inv * (d_normed * gain_ref[:, cols] - x_hat * mean)
            if last:
                out_rows[:, cols] = (cv[:, cols].astype(F32) + change).astype(BF)
            else:
                rest[:, cols] = change
            return carry

        lax.fori_loop(0, N_CH, body, 0, unroll=UNROLL)

    @pl.when(sec == 1)
    def _():
        half_load(1).start()
        half_load(0).start()
        wu_load.start()

        def greet(i, carry):
            pl.semaphore_signal(barrier, inc=1, device_id=(0, peer_at(i)), device_id_type=MESH)
            return carry

        lax.fori_loop(0, N_PEER, greet, 0)
        routes_load.start()
        counts_load.start()
        gain_load.start()
        wd_load.start()
        half_load(1).wait()
        arrange(1)
        half_load(0).wait()
        wu_load.wait()
        arrange_early()
        pl.semaphore_wait(barrier, 1)
        send_early()
        pltpu.make_async_copy(a2a_send.at[me], a2a_recv.at[1, 0], own_sem.at[1]).start()
        send_rows(1)
        routes_load.wait()
        counts_load.wait()
        choose()
        gain_load.wait()
        wd_load.wait()
        inv, hidden, gate, _ = forward(True)
        pick(0)
        lax.fori_loop(0, N_CH, turn_rows, 0, unroll=UNROLL)
        d_hidden = hidden_grad(early_active(), hidden, gate)
        make_down(d_hidden, inv)
        pick(1)
        row_pass(d_hidden, hidden, inv, False)
        pick(2)
        pick(3)
        make_up()

    @pl.when(sec == 0)
    def _():
        half_load(0).start()
        x_load.start()
        gain_load.start()
        wd_load.start()
        wu_load.start()
        for axis in range(3):
            for step in range(1, 4):
                pl.semaphore_signal(barrier, inc=1, device_id=along(axis, step), device_id_type=MESH)
        half_load(0).wait()
        arrange(0)
        pl.semaphore_wait(barrier, N_PEER + 9)
        pl.semaphore_signal(barrier, inc=1, device_id=partner, device_id_type=MESH)
        send_rows(0)
        x_load.wait()
        gain_load.wait()
        wd_load.wait()
        inv, hidden, gate, active = forward(False)
        wu_load.wait()

        def up(c, carry):
            y = jnp.dot(active, wu_v[:, cols_of(c)], preferred_element_type=F32)
            fo[:, cols_of(c)] = (x_v[:, cols_of(c)].astype(F32) + y).astype(BF)
            rcopy(
                fo.at[:, cols_of(c)], x_v.at[:, cols_of(c)], row_ssem.at[c], row_rsem.at[c], partner
            ).start()
            return carry

        lax.fori_loop(0, N_CH, up, 0, unroll=UNROLL)
        lax.fori_loop(0, N_CH, turn_rows, 0, unroll=UNROLL)

        def body(c, acc):
            row_wait(cv, c).wait_recv()
            return acc + lax.dot_general(
                cv[:, cols_of(c)], wu_v[:, cols_of(c)], INNER, preferred_element_type=F32
            )

        d_active = lax.fori_loop(0, N_CH, body, jnp.zeros((ROWS, R), F32), unroll=UNROLL)
        d_hidden = hidden_grad(d_active, hidden, gate)
        make_down(d_hidden, inv)
        make_up()
        row_pass(d_hidden, hidden, inv, True)

    def gain_send(stage):
        axis = 2 - stage
        for step in range(1, 4):
            rcopy(
                gg.at[stage], gin.at[stage, step - 1], gain_ssem, gain_rsem.at[stage], along(axis, step)
            ).start()

    def gain_add(stage):
        wait_recv(gin.at[stage], (gain_ssem, gain_rsem.at[stage]), partner)
        gg[stage + 1] = gg[stage] + gin[stage, 0] + gin[stage, 1] + gin[stage, 2]

    gain_send(0)
    both = (1, 0)
    for t in both:
        stage1_merge(t)
    gain_add(0)
    gain_send(1)
    for t in both:
        stage2_send(t)
    gain_add(1)
    gain_send(2)
    for t in both:
        stage3_send(t)
    gain_add(2)
    out_gain[...] = (gg[3] * FACTOR).astype(BF)
    for t in both:
        gather2_send(t)
    for t in both:
        gather3_send(t)
    for t in both:
        relay_send(t)
    for t in both:
        finish(t)

    wait_send(gin, (gain_ssem, gain_rsem.at[0]), partner)

    @pl.when(sec == 0)
    def _():
        rcopy(a2a_send, a2a_send, a2a_ssem, early_rsem, partner).wait_send()

        def sent(c, carry):
            row_wait(fo, c).wait_send()
            return carry

        lax.fori_loop(0, N_CH, sent, 0)

    @pl.when(sec == 1)
    def _():
        for sent_from, sem in ((a2a_send, a2a_ssem), (early_send, early_ssem)):
            others = sent_from.at[pl.ds(0, N_PEER - 1)]
            rcopy(others, others, sem, early_rsem, partner).wait_send()

        def sent(c, carry):
            row_wait(out_rows, c).wait_send()
            return carry

        lax.fori_loop(0, N_CH, sent, 0)


def both_kinds(lead):
    ups = [pltpu.VMEM((*lead, 16, w), BF) for w in UP_W]
    downs = [pltpu.VMEM((*lead, h, R), BF) for h in DN_H]
    return ups + downs


def write_out(*refs):
    n = (len(refs) - 1) // 2
    sem = refs[-1]
    copies = [pltpu.make_async_copy(refs[i], refs[n + i], sem.at[i]) for i in range(n)]
    for copy in copies:
        copy.start()
    for copy in copies:
        copy.wait()


def stay(operand):
    return pltpu.with_memory_space_constraint(operand, pltpu.HBM)


def shards(inputs, routes, counts, cotangent, gain_vector, w_down, w_up):
    hbm = pl.BlockSpec(memory_space=pltpu.HBM)
    vmem = pl.BlockSpec(memory_space=pltpu.VMEM)
    anywhere = pl.BlockSpec(memory_space=pl.ANY)
    dma = pltpu.SemaphoreType.DMA
    scratch = [
        pltpu.VMEM((ROWS, D), BF),
        pltpu.VMEM((1, ROWS), jnp.int32),
        pltpu.VMEM((1, 1), jnp.int32),
        pltpu.VMEM((1, D), F32),
        pltpu.VMEM((D, R), BF),
        pltpu.VMEM((R, D), BF),
        pltpu.VMEM((SLOTS, D), BF),
        pltpu.VMEM((N_PEER, 16, QUART), BF),
        pltpu.VMEM((2, N_PEER, 16, QUART), BF),
        pltpu.VMEM((N_PEER, 16, 128), BF),
        pltpu.VMEM((N_PEER, 16, 128), BF),
        pltpu.VMEM((RING, 16, 80, ROWS), BF),
        pltpu.VMEM((ROWS, D), BF),
        pltpu.VMEM((ROWS, D), BF),
        pltpu.VMEM((ROWS, D), F32),
        pltpu.VMEM((4 * ROWS, N_PEER * 16), BF),
        pltpu.VMEM((R, ROWS), BF),
    ]
    for lead in ((4, 4, 4), (2, 2, 4), (2, 4, 4), (4, 4), (3, 4), (4, 4)):
        scratch += both_kinds(lead)
    scratch += [
        pltpu.VMEM((4, 1, D), F32),
        pltpu.VMEM((3, 3, 1, D), F32),
        dma((8,)),
        dma((2,)),
        dma,
        dma((2, N_GROUP)),
        dma,
        dma,
        dma((N_CH,)),
        dma((N_CH,)),
        dma((2, 3)),
        dma((2, 3, 10)),
        dma,
        dma((3,)),
    ]
    shapes = [(1, D), (RING, RING, RING, 80, R), (RING, RING, 16, D), (ROWS, D)]
    made = pl.pallas_call(
        kernel,
        out_shape=[pltpu.VMEM(s, BF) for s in shapes],
        in_specs=[hbm, anywhere, anywhere, hbm, hbm, hbm, hbm],
        out_specs=[vmem] * 4,
        scratch_shapes=scratch,
        compiler_params=pltpu.CompilerParams(
            collective_id=0, has_side_effects=True, vmem_limit_bytes=44 * 2**20
        ),
    )(
        stay(inputs), stay(routes.reshape(1, ROWS)), counts.reshape(1, 1), stay(cotangent), stay(gain_vector),
        stay(w_down), stay(w_up),
    )
    gain, down, up, rows = pl.pallas_call(
        write_out,
        out_shape=[jax.ShapeDtypeStruct(s, BF) for s in shapes],
        in_specs=[vmem] * 4,
        out_specs=[hbm] * 4,
        scratch_shapes=[dma((4,))],
        compiler_params=pltpu.CompilerParams(vmem_limit_bytes=2**20),
    )(*made)
    return gain, down.reshape(1, D, R), up.reshape(1, R, D), rows[None]


def solution(mesh):
    in_specs = (
        P("peer", None),
        P("peer", None),
        P("peer"),
        P("peer", None, None),
        P("section", None),
        P("section", None, None),
        P("section", None, None),
    )
    out_specs = (
        P("section", None),
        P("section", None, None),
        P("section", None, None),
        P("section", "peer", None),
    )
    return jax.shard_map(shards, mesh=mesh, in_specs=in_specs, out_specs=out_specs, check_vma=False)
```

```python
import jax
import jax.numpy as jnp
from jax import lax
from jax.experimental import pallas as pl
from jax.experimental.pallas import tpu as pltpu
from jax.sharding import PartitionSpec as P

rms_eps = 1e-05
MESH = pl.DeviceIdType.MESH
BF = jnp.bfloat16
F32 = jnp.float32

ROWS, D, R = 128, 5120, 256
SLOTS, CAP = 256, 4
N_PEER, RING = 64, 4
HALF = D // 2
QUART = HALF // 4
GROUP = 16
N_GROUP = N_PEER // GROUP
UNROLL = 4
CH = 640
N_CH = D // CH
ACOL = D // RING
UP_OFF, UP_W = (0, 384, 768), (384, 384, 512)
DN_OFF, DN_H = (0, 32, 64), (32, 32, 16)
ORDER = ((0, 1, 2), (1, 2, 0), (2, 0, 1))
FACTOR = float(N_PEER * ROWS) ** (-0.5)
INNER = (((1,), (1,)), ((), ()))


def mod4(v):
    return lax.rem(v + 8, 4)


def rcopy(src, dst, send_sem, recv_sem, device):
    return pltpu.make_async_remote_copy(
        src_ref=src,
        dst_ref=dst,
        send_sem=send_sem,
        recv_sem=recv_sem,
        device_id=device,
        device_id_type=MESH,
    )


def wait_recv(dst, sems, device):
    rcopy(dst, dst, sems[0], sems[1], device).wait_recv()


def wait_send(src, sems, device):
    rcopy(src, src, sems[0], sems[1], device).wait_send()


def kernel(
    x_hbm, routes_hbm, counts_hbm, cot_hbm, gain_hbm, wd_hbm, wu_hbm,
    out_gain, out_dn, out_up, out_rows,
    x_v, routes_ref, counts_ref, gain_ref, wd_v, wu_v, cot_v, a2a_send, a2a_recv, early_send, early_recv, nt, cv, fo, rest, sel, act_t,
    gu0, gu1, gu2, gd0, gd1, gd2,
    ru0, ru1, ru2, rd0, rd1, rd2,
    iu0, iu1, iu2, id0, id1, id2,
    su0, su1, su2, sd0, sd1, sd2,
    i2u0, i2u1, i2u2, i2d0, i2d1, i2d2,
    s2u0, s2u1, s2u2, s2d0, s2d1, s2d2,
    i3u0, i3u1, i3u2, i3d0, i3d1, i3d2,
    gg, gin,
    load_sem, own_sem, a2a_ssem, a2a_rsem, early_ssem, early_rsem, row_ssem, row_rsem, red_ssem, red_rsem, gain_ssem, gain_rsem,
):
    grad = ((gu0, gu1, gu2), (gd0, gd1, gd2))
    rly = ((ru0, ru1, ru2), (rd0, rd1, rd2))
    inb = ((iu0, iu1, iu2), (id0, id1, id2))
    s1 = ((su0, su1, su2), (sd0, sd1, sd2))
    in2 = ((i2u0, i2u1, i2u2), (i2d0, i2d1, i2d2))
    s2 = ((s2u0, s2u1, s2u2), (s2d0, s2d1, s2d2))
    in3 = ((i3u0, i3u1, i3u2), (i3d0, i3d1, i3d2))

    sec = lax.axis_index("section")
    me = lax.axis_index("peer")
    pos = (me // 16, lax.rem(me // 4, 4), lax.rem(me, 4))
    weight = (16, 4, 1)

    def along(axis, step):
        there = mod4(pos[axis] + step)
        return (sec, me + (there - pos[axis]) * weight[axis])

    partner = (1 - sec, me)

    def half_load(h):
        cols = pl.ds(h * HALF, HALF)
        return pltpu.make_async_copy(cot_hbm.at[0, :, cols], cot_v.at[:, cols], load_sem.at[h])

    wd_load = pltpu.make_async_copy(wd_hbm.at[0], wd_v, load_sem.at[2])
    wu_load = pltpu.make_async_copy(wu_hbm.at[0], wu_v, load_sem.at[3])
    x_load = pltpu.make_async_copy(x_hbm, x_v, load_sem.at[4])
    gain_load = pltpu.make_async_copy(gain_hbm, gain_ref, load_sem.at[5])
    routes_load = pltpu.make_async_copy(routes_hbm, routes_ref, load_sem.at[6])
    counts_load = pltpu.make_async_copy(counts_hbm, counts_ref, load_sem.at[7])
    barrier = pltpu.get_barrier_semaphore()

    def cols_of(c):
        return pl.ds(pl.multiple_of(c * CH, CH), CH)

    def blocks(quarters, width):
        o_i = lax.broadcasted_iota(jnp.int32, (SLOTS, SLOTS), 0)
        i_i = lax.broadcasted_iota(jnp.int32, (SLOTS, SLOTS), 1)
        perm = jnp.where(i_i == (o_i & 3) * 64 + (o_i >> 2), 1.0, 0.0).astype(BF)
        moved = jnp.dot(perm, jnp.concatenate(quarters, axis=0), preferred_element_type=F32)
        return moved.astype(BF).reshape(16, 16, width)

    def arrange(h):
        for g in range(4):
            rows = slice(g * 64, (g + 1) * 64)
            starts = [h * HALF + j * QUART for j in range(4)]
            a2a_send[g * 16:(g + 1) * 16] = blocks([cot_v[rows, lo:lo + QUART] for lo in starts], QUART)

    def peer_at(i):
        i2, i1, i0 = i // 16, lax.rem(i // 4, 4), lax.rem(i, 4)
        return mod4(pos[0] + i2 + i0) * 16 + mod4(pos[1] + i1 + i0) * 4 + mod4(pos[2] + i0)

    def send_rows(h):
        def send(i, carry):
            dst = peer_at(i)
            rcopy(
                a2a_send.at[dst], a2a_recv.at[h, i], a2a_ssem, a2a_rsem.at[h, i // GROUP], (1, dst)
            ).start()
            return carry

        lax.fori_loop(h, N_PEER, send, 0)

    def arrange_early():
        def body(c, acc):
            return acc + lax.dot_general(
                cot_v[:, cols_of(c)], wu_v[:, cols_of(c)], INNER, preferred_element_type=F32
            )

        d_slot = lax.fori_loop(0, N_CH, body, jnp.zeros((SLOTS, R), F32), unroll=UNROLL)
        high = d_slot.astype(BF)
        low = (d_slot - high.astype(F32)).astype(BF)
        for g in range(4):
            rows = slice(g * 64, (g + 1) * 64)
            early_send[g * 16:(g + 1) * 16] = blocks(
                [part[rows, lo:lo + 128] for part in (high, low) for lo in (0, 128)], 128
            )

    def send_early():
        pltpu.make_async_copy(early_send.at[me], early_recv.at[0], own_sem.at[0]).start()

        def send(i, carry):
            dst = peer_at(i)
            rcopy(early_send.at[dst], early_recv.at[i], early_ssem, early_rsem, (1, dst)).start()
            return carry

        lax.fori_loop(1, N_PEER, send, 0)

    def row_wait(ref, c):
        return rcopy(ref.at[:, cols_of(c)], ref.at[:, cols_of(c)], row_ssem.at[c], row_rsem.at[c], partner)

    def scaled(c):
        return (x_v[:, cols_of(c)].astype(F32) * gain_ref[:, cols_of(c)]).astype(BF)

    def turn_rows(c, carry):
        half = pl.ds(pl.multiple_of(lax.rem(c, 2) * 8, 8), 8)
        nt[c // 2, half] = scaled(c).T.reshape(8, 80, ROWS)
        return carry

    def forward(arriving):
        def down(c, carry):
            raw, total = carry
            if arriving:
                row_wait(x_v, c).wait_recv()
            xf = x_v[:, cols_of(c)].astype(F32)
            total = total + jnp.sum(xf * xf, axis=1, keepdims=True)
            return raw + jnp.dot(scaled(c), wd_v[cols_of(c), :], preferred_element_type=F32), total

        start = jnp.zeros((ROWS, R), F32), jnp.zeros((ROWS, 1), F32)
        raw, total = lax.fori_loop(0, N_CH, down, start, unroll=UNROLL)
        inv = lax.rsqrt(total / D + rms_eps)
        hidden = raw * inv
        gate = jax.nn.sigmoid(hidden)
        active = (hidden * gate).astype(BF)
        act_t[...] = active.T
        return inv, hidden, gate, active

    def choose():
        dest = routes_ref[...]
        live = lax.broadcasted_iota(jnp.int32, (1, ROWS), 1) < counts_ref[...]
        lane = lax.broadcasted_iota(jnp.int32, (ROWS, ROWS), 1)
        row = lax.broadcasted_iota(jnp.int32, (ROWS, ROWS), 0)
        named = jnp.where((row == dest) & live, 1.0, 0.0)
        before = jnp.where(row < lane, 1.0, 0.0).astype(BF)
        rank = jnp.dot(named.astype(BF), before, preferred_element_type=F32)
        nth = jnp.sum(named * rank, axis=0, keepdims=True)
        z = (pos[2] + 4 - (dest & 3)) & 3
        x = (pos[1] + 8 - ((dest >> 2) & 3) - z) & 3
        y = (pos[0] + 8 - (dest >> 4) - z) & 3
        turn = y * 16 + x * 4 + z
        across = jnp.where(live, turn.astype(F32) * 16.0 + nth * 4.0, -16.0)
        place = jnp.sum(jnp.where(row == lane, across, 0.0), axis=1, keepdims=True)
        column = lax.broadcasted_iota(jnp.int32, (ROWS, N_PEER * 16), 1).astype(F32)
        for j in range(4):
            sel[j * ROWS:(j + 1) * ROWS, :] = jnp.where(column == place + float(j), 1.0, 0.0).astype(BF)

    def early_active():
        pltpu.make_async_copy(early_send.at[me], early_recv.at[0], own_sem.at[0]).wait()
        others = early_recv.at[pl.ds(1, N_PEER - 1)]
        rcopy(others, others, early_ssem, early_rsem, partner).wait_recv()
        got = jnp.dot(
            sel[...], early_recv[...].reshape(N_PEER * 16, 128), preferred_element_type=F32
        ).reshape(4, ROWS, 128)
        return jnp.concatenate([got[0] + got[2], got[1] + got[3]], axis=1)

    def pick(g):
        group = pl.ds(g * GROUP, GROUP)
        for h in range(2):
            landed = a2a_recv.at[h, group]
            if h == 1 and g == 0:
                pltpu.make_async_copy(a2a_send.at[me], a2a_recv.at[1, 0], own_sem.at[1]).wait()
                landed = a2a_recv.at[1, pl.ds(1, GROUP - 1)]
            rcopy(landed, landed, a2a_ssem, a2a_rsem.at[h, g], partner).wait_recv()
            picked = jnp.dot(
                sel[:, g * GROUP * 16:(g + 1) * GROUP * 16],
                a2a_recv[h, group].reshape(GROUP * 16, QUART),
                preferred_element_type=F32,
            ).astype(BF)
            for j in range(4):
                cols = pl.ds((h * 4 + j) * CH, CH)
                part = picked[j * ROWS:(j + 1) * ROWS, :]
                if g > 0:
                    part = cv[:, cols] + part
                cv[:, cols] = part
                if g == N_GROUP - 1:
                    out_rows[:, cols] = (part.astype(F32) + rest[:, cols]).astype(BF)
                    rcopy(
                        out_rows.at[:, cols], cv.at[:, cols],
                        row_ssem.at[h * 4 + j], row_rsem.at[h * 4 + j], partner,
                    ).start()

    def out_at(t, k, a, b, c):
        if t == 0:
            cols = pl.ds(pl.multiple_of(a * ACOL + UP_OFF[k], 128), UP_W[k])
            return out_up.at[b, c, :, cols]
        return out_dn.at[a, b, c, pl.ds(DN_OFF[k], DN_H[k]), :]

    every = pl.ds(0, RING)
    lower, upper = pl.ds(0, 2), pl.ds(2, 2)

    def sems(t, k, i):
        return red_ssem.at[t, k], red_rsem.at[t, k, i]

    def ship(src, dst, t, k, i, device):
        rcopy(src, dst, *sems(t, k, i), device).start()

    def here(dst, t, k, i):
        wait_recv(dst, sems(t, k, i), partner)

    def first_axis(k):
        return pos[ORDER[k][0]]

    def sides(k):
        axis = ORDER[k][0]
        return along(axis, -1), along(axis, 1)

    def stage1_send(t):
        for k in range(3):
            g, left, right = grad[t][k], *sides(k)
            ship(g.at[2, lower], rly[t][k].at[0], t, k, 0, right)
            ship(g.at[2, upper], rly[t][k].at[1], t, k, 1, left)
            ship(g.at[1, upper], inb[t][k].at[0, upper], t, k, 2, right)
            ship(g.at[3, lower], inb[t][k].at[1, lower], t, k, 2, left)

    def stage1_merge(t):
        for k in range(3):
            g, left, right = grad[t][k], *sides(k)
            here(rly[t][k].at[0], t, k, 0)
            g[1, 0:2] = (g[1, 0:2].astype(F32) + rly[t][k][0].astype(F32)).astype(BF)
            ship(g.at[1, lower], inb[t][k].at[0, lower], t, k, 2, right)
            here(rly[t][k].at[1], t, k, 1)
            g[3, 2:4] = (g[3, 2:4].astype(F32) + rly[t][k][1].astype(F32)).astype(BF)
            ship(g.at[3, upper], inb[t][k].at[1, upper], t, k, 2, left)

    def stage2_send(t):
        for k in range(3):
            g, box, part = grad[t][k], inb[t][k], s1[t][k]
            here(box, t, k, 2)

            def add(b, carry, g=g, box=box, part=part):
                part[b] = (g[0, b].astype(F32) + box[0, b].astype(F32) + box[1, b].astype(F32)).astype(BF)
                return carry

            lax.fori_loop(0, RING, add, 0)
            axis = ORDER[k][1]
            for step in range(1, 4):
                ship(part.at[mod4(pos[axis] + step)], in2[t][k].at[step - 1], t, k, 3, along(axis, step))

    def line_sum(t, k):
        box = in2[t][k]
        here(box, t, k, 3)
        mine = s1[t][k][pos[ORDER[k][1]]].astype(F32)
        return (mine + box[0].astype(F32) + box[1].astype(F32) + box[2].astype(F32)).astype(BF)

    def stage3_send(t):
        @pl.when(sec == 0)
        def _():
            for k in range(3):
                axis = ORDER[k][2]
                part = in3[t][k].at[pos[axis]]
                part[...] = line_sum(t, k)
                for step in range(1, 4):
                    ship(part, part, t, k, 4, along(axis, step))

        @pl.when(sec == 1)
        def _():
            for k in range(3):
                axis = ORDER[k][2]
                part = s2[t][k]
                part[...] = line_sum(t, k)
                for step in range(1, 4):
                    ship(part.at[mod4(pos[axis] + step)], in3[t][k].at[0, step - 1], t, k, 4, along(axis, step))

    def gather1_send(t):
        @pl.when(sec == 1)
        def _():
            for k in range(3):
                a, b, c = (pos[axis] for axis in ORDER[k])
                box = in3[t][k].at[0]
                here(box.at[0:3], t, k, 4)
                mine = s2[t][k][c].astype(F32)
                whole = mine + box[0].astype(F32) + box[1].astype(F32) + box[2].astype(F32)
                piece = out_at(t, k, a, b, c)
                piece[...] = (whole * FACTOR).astype(BF)
                for step in range(1, 4):
                    ship(piece, piece, t, k, 5, along(ORDER[k][2], step))

    def gather2_send(t):
        for k in range(3):
            a, b, _ = (pos[axis] for axis in ORDER[k])
            box = in3[t][k]
            mine = out_at(t, k, a, b, every)

            @pl.when(sec == 0)
            def _(k=k, box=box, mine=mine):
                here(box.at[0:3], t, k, 4)
                whole = box[0].astype(F32) + box[1].astype(F32) + box[2].astype(F32) + box[3].astype(F32)
                mine[...] = (whole * FACTOR).astype(BF)

            @pl.when(sec == 1)
            def _(k=k, box=box):
                here(box.at[0, 0:3], t, k, 5)

            axis = ORDER[k][1]
            for step in range(1, 4):
                ship(mine, mine, t, k, 6, along(axis, step))

    def gather3_send(t):
        for k in range(3):
            here(in2[t][k], t, k, 6)
            left, right = sides(k)
            a = first_axis(k)
            low, high = out_at(t, k, a, lower, every), out_at(t, k, a, upper, every)
            ship(low, low, t, k, 7, right)
            ship(high, high, t, k, 8, left)
            ship(high, high, t, k, 9, right)
            ship(low, low, t, k, 9, left)

    def relay_send(t):
        for k in range(3):
            a = first_axis(k)
            left, right = sides(k)
            part = out_at(t, k, mod4(a - 1), lower, every)
            here(part, t, k, 7)
            ship(part, part, t, k, 9, right)
            part = out_at(t, k, mod4(a + 1), upper, every)
            here(part, t, k, 8)
            ship(part, part, t, k, 9, left)

    def finish(t):
        for k in range(3):
            here(inb[t][k], t, k, 9)
            g = grad[t][k]

            @pl.when(sec == 0)
            def _(k=k, g=g):
                for sent in (g, g, g.at[0, 0]):
                    wait_send(sent, sems(t, k, 0), partner)

            @pl.when(sec == 1)
            def _(k=k, g=g):
                for sent in (g, g.at[0:3], g.at[3, 0:3], g.at[3, 3, 0:2]):
                    wait_send(sent, sems(t, k, 0), partner)

    def make_up():
        def body(j, carry):
            for k in range(3):
                a = mod4(first_axis(k) + j)
                cols = pl.ds(pl.multiple_of(a * ACOL + UP_OFF[k], 128), UP_W[k])
                g = jnp.dot(act_t[...], cv[:, cols], preferred_element_type=F32)
                grad[0][k][j] = g.astype(BF).reshape(4, 4, 16, UP_W[k])
            return carry

        lax.fori_loop(0, RING, body, 0, unroll=UNROLL)
        stage1_send(0)

    def make_down(d_hidden, inv):
        d_scaled = (d_hidden * inv).astype(BF)

        def body(j, carry):
            for k in range(3):
                a = mod4(first_axis(k) + j)
                h = DN_H[k]
                lhs = nt[a, :, DN_OFF[k]:DN_OFF[k] + h, :].reshape(16 * h, ROWS)
                g = jnp.dot(lhs, d_scaled, preferred_element_type=F32)
                grad[1][k][j] = g.astype(BF).reshape(4, 4, h, R)
            return carry

        lax.fori_loop(0, RING, body, 0, unroll=UNROLL)
        stage1_send(1)

    def hidden_grad(d_active, hidden, gate):
        return d_active * gate * (1.0 + hidden * (1.0 - gate))

    def row_pass(d_hidden, hidden, inv, last):
        d_hidden = d_hidden.astype(BF)
        mean = jnp.sum(d_hidden.astype(F32) * hidden, axis=1, keepdims=True) / D

        def body(c, carry):
            cols = cols_of(c)
            d_normed = lax.dot_general(d_hidden, wd_v[cols, :], INNER, preferred_element_type=F32)
            x_hat = x_v[:, cols].astype(F32) * inv
            gg[0, :, cols] = jnp.sum(d_normed * x_hat, axis=0, keepdims=True)
            change = inv * (d_normed * gain_ref[:, cols] - x_hat * mean)
            if last:
                out_rows[:, cols] = (cv[:, cols].astype(F32) + change).astype(BF)
            else:
                rest[:, cols] = change
            return carry

        lax.fori_loop(0, N_CH, body, 0, unroll=UNROLL)

    @pl.when(sec == 1)
    def _():
        half_load(1).start()
        half_load(0).start()
        wu_load.start()

        def greet(i, carry):
            pl.semaphore_signal(barrier, inc=1, device_id=(0, peer_at(i)), device_id_type=MESH)
            return carry

        lax.fori_loop(0, N_PEER, greet, 0)
        routes_load.start()
        counts_load.start()
        gain_load.start()
        wd_load.start()
        half_load(1).wait()
        arrange(1)
        half_load(0).wait()
        wu_load.wait()
        arrange_early()
        pl.semaphore_wait(barrier, 1)
        send_early()
        pltpu.make_async_copy(a2a_send.at[me], a2a_recv.at[1, 0], own_sem.at[1]).start()
        send_rows(1)
        routes_load.wait()
        counts_load.wait()
        choose()
        gain_load.wait()
        wd_load.wait()
        inv, hidden, gate, _ = forward(True)
        pick(0)
        lax.fori_loop(0, N_CH, turn_rows, 0, unroll=UNROLL)
        d_hidden = hidden_grad(early_active(), hidden, gate)
        make_down(d_hidden, inv)
        pick(1)
        row_pass(d_hidden, hidden, inv, False)
        pick(2)
        pick(3)
        make_up()

    @pl.when(sec == 0)
    def _():
        half_load(0).start()
        x_load.start()
        gain_load.start()
        wd_load.start()
        wu_load.start()
        for axis in range(3):
            for step in range(1, 4):
                pl.semaphore_signal(barrier, inc=1, device_id=along(axis, step), device_id_type=MESH)
        half_load(0).wait()
        arrange(0)
        pl.semaphore_wait(barrier, N_PEER + 9)
        pl.semaphore_signal(barrier, inc=1, device_id=partner, device_id_type=MESH)
        send_rows(0)
        x_load.wait()
        gain_load.wait()
        wd_load.wait()
        inv, hidden, gate, active = forward(False)
        wu_load.wait()

        def up(c, carry):
            y = jnp.dot(active, wu_v[:, cols_of(c)], preferred_element_type=F32)
            fo[:, cols_of(c)] = (x_v[:, cols_of(c)].astype(F32) + y).astype(BF)
            rcopy(
                fo.at[:, cols_of(c)], x_v.at[:, cols_of(c)], row_ssem.at[c], row_rsem.at[c], partner
            ).start()
            return carry

        lax.fori_loop(0, N_CH, up, 0, unroll=UNROLL)
        lax.fori_loop(0, N_CH, turn_rows, 0, unroll=UNROLL)

        def body(c, acc):
            row_wait(cv, c).wait_recv()
            return acc + lax.dot_general(
                cv[:, cols_of(c)], wu_v[:, cols_of(c)], INNER, preferred_element_type=F32
            )

        d_active = lax.fori_loop(0, N_CH, body, jnp.zeros((ROWS, R), F32), unroll=UNROLL)
        d_hidden = hidden_grad(d_active, hidden, gate)
        make_down(d_hidden, inv)
        make_up()
        row_pass(d_hidden, hidden, inv, True)

    def gain_send(stage):
        axis = 2 - stage
        for step in range(1, 4):
            rcopy(
                gg.at[stage], gin.at[stage, step - 1], gain_ssem, gain_rsem.at[stage], along(axis, step)
            ).start()

    def gain_add(stage):
        wait_recv(gin.at[stage], (gain_ssem, gain_rsem.at[stage]), partner)
        gg[stage + 1] = gg[stage] + gin[stage, 0] + gin[stage, 1] + gin[stage, 2]

    gain_send(0)
    both = (1, 0)
    for t in both:
        stage1_merge(t)
    gain_add(0)
    gain_send(1)
    for t in both:
        stage2_send(t)
    gain_add(1)
    gain_send(2)
    for t in both:
        stage3_send(t)
    gain_add(2)
    out_gain[...] = (gg[3] * FACTOR).astype(BF)
    for t in both:
        gather1_send(t)
    for t in both:
        gather2_send(t)
    for t in both:
        gather3_send(t)
    for t in both:
        relay_send(t)
    for t in both:
        finish(t)

    wait_send(gin, (gain_ssem, gain_rsem.at[0]), partner)

    @pl.when(sec == 0)
    def _():
        rcopy(a2a_send, a2a_send, a2a_ssem, early_rsem, partner).wait_send()

        def sent(c, carry):
            row_wait(fo, c).wait_send()
            return carry

        lax.fori_loop(0, N_CH, sent, 0)

    @pl.when(sec == 1)
    def _():
        for sent_from, sem in ((a2a_send, a2a_ssem), (early_send, early_ssem)):
            others = sent_from.at[pl.ds(0, N_PEER - 1)]
            rcopy(others, others, sem, early_rsem, partner).wait_send()

        def sent(c, carry):
            row_wait(out_rows, c).wait_send()
            return carry

        lax.fori_loop(0, N_CH, sent, 0)


def both_kinds(lead):
    ups = [pltpu.VMEM((*lead, 16, w), BF) for w in UP_W]
    downs = [pltpu.VMEM((*lead, h, R), BF) for h in DN_H]
    return ups + downs


def write_out(*refs):
    n = (len(refs) - 1) // 2
    sem = refs[-1]
    copies = [pltpu.make_async_copy(refs[i], refs[n + i], sem.at[i]) for i in range(n)]
    for copy in copies:
        copy.start()
    for copy in copies:
        copy.wait()


def stay(operand):
    return pltpu.with_memory_space_constraint(operand, pltpu.HBM)


def shards(inputs, routes, counts, cotangent, gain_vector, w_down, w_up):
    hbm = pl.BlockSpec(memory_space=pltpu.HBM)
    vmem = pl.BlockSpec(memory_space=pltpu.VMEM)
    anywhere = pl.BlockSpec(memory_space=pl.ANY)
    dma = pltpu.SemaphoreType.DMA
    scratch = [
        pltpu.VMEM((ROWS, D), BF),
        pltpu.VMEM((1, ROWS), jnp.int32),
        pltpu.VMEM((1, 1), jnp.int32),
        pltpu.VMEM((1, D), F32),
        pltpu.VMEM((D, R), BF),
        pltpu.VMEM((R, D), BF),
        pltpu.VMEM((SLOTS, D), BF),
        pltpu.VMEM((N_PEER, 16, QUART), BF),
        pltpu.VMEM((2, N_PEER, 16, QUART), BF),
        pltpu.VMEM((N_PEER, 16, 128), BF),
        pltpu.VMEM((N_PEER, 16, 128), BF),
        pltpu.VMEM((RING, 16, 80, ROWS), BF),
        pltpu.VMEM((ROWS, D), BF),
        pltpu.VMEM((ROWS, D), BF),
        pltpu.VMEM((ROWS, D), F32),
        pltpu.VMEM((4 * ROWS, N_PEER * 16), BF),
        pltpu.VMEM((R, ROWS), BF),
    ]
    for lead in ((4, 4, 4), (2, 2, 4), (2, 4, 4), (4, 4), (3, 4), (4,), (4, 4)):
        scratch += both_kinds(lead)
    scratch += [
        pltpu.VMEM((4, 1, D), F32),
        pltpu.VMEM((3, 3, 1, D), F32),
        dma((8,)),
        dma((2,)),
        dma,
        dma((2, N_GROUP)),
        dma,
        dma,
        dma((N_CH,)),
        dma((N_CH,)),
        dma((2, 3)),
        dma((2, 3, 10)),
        dma,
        dma((3,)),
    ]
    shapes = [(1, D), (RING, RING, RING, 80, R), (RING, RING, 16, D), (ROWS, D)]
    made = pl.pallas_call(
        kernel,
        out_shape=[pltpu.VMEM(s, BF) for s in shapes],
        in_specs=[hbm, anywhere, anywhere, hbm, hbm, hbm, hbm],
        out_specs=[vmem] * 4,
        scratch_shapes=scratch,
        compiler_params=pltpu.CompilerParams(
            collective_id=0, has_side_effects=True, vmem_limit_bytes=44 * 2**20
        ),
    )(
        stay(inputs), stay(routes.reshape(1, ROWS)), counts.reshape(1, 1), stay(cotangent), stay(gain_vector),
        stay(w_down), stay(w_up),
    )
    gain, down, up, rows = pl.pallas_call(
        write_out,
        out_shape=[jax.ShapeDtypeStruct(s, BF) for s in shapes],
        in_specs=[vmem] * 4,
        out_specs=[hbm] * 4,
        scratch_shapes=[dma((4,))],
        compiler_params=pltpu.CompilerParams(vmem_limit_bytes=2**20),
    )(*made)
    return gain, down.reshape(1, D, R), up.reshape(1, R, D), rows[None]


def solution(mesh):
    in_specs = (
        P("peer", None),
        P("peer", None),
        P("peer"),
        P("peer", None, None),
        P("section", None),
        P("section", None, None),
        P("section", None, None),
    )
    out_specs = (
        P("section", None),
        P("section", None, None),
        P("section", None, None),
        P("section", "peer", None),
    )
    return jax.shard_map(shards, mesh=mesh, in_specs=in_specs, out_specs=out_specs, check_vma=False)
```

```python
import jax
import jax.numpy as jnp
from jax import lax
from jax.experimental import pallas as pl
from jax.experimental.pallas import tpu as pltpu
from jax.sharding import PartitionSpec as P

rms_eps = 1e-05
MESH = pl.DeviceIdType.MESH
BF = jnp.bfloat16
F32 = jnp.float32

ROWS, D, R = 128, 5120, 256
SLOTS, CAP = 256, 4
N_PEER, RING = 64, 4
HALF = D // 2
QUART = HALF // 4
GROUP = 16
N_GROUP = N_PEER // GROUP
UNROLL = 4
CH = 640
N_CH = D // CH
ACOL = D // RING
UP_OFF, UP_W = (0, 384, 768), (384, 384, 512)
DN_OFF, DN_H = (0, 32, 64), (32, 32, 16)
ORDER = ((0, 1, 2), (1, 2, 0), (2, 0, 1))
FACTOR = float(N_PEER * ROWS) ** (-0.5)
INNER = (((1,), (1,)), ((), ()))


def mod4(v):
    return lax.rem(v + 8, 4)


def rcopy(src, dst, send_sem, recv_sem, device):
    return pltpu.make_async_remote_copy(
        src_ref=src,
        dst_ref=dst,
        send_sem=send_sem,
        recv_sem=recv_sem,
        device_id=device,
        device_id_type=MESH,
    )


def wait_recv(dst, sems, device):
    rcopy(dst, dst, sems[0], sems[1], device).wait_recv()


def wait_send(src, sems, device):
    rcopy(src, src, sems[0], sems[1], device).wait_send()


def kernel(
    x_hbm, routes_hbm, counts_hbm, cot_hbm, gain_hbm, wd_hbm, wu_hbm,
    out_gain, out_dn, out_up, out_rows,
    x_v, routes_ref, counts_ref, gain_ref, wd_v, wu_v, cot_v, a2a_send, a2a_recv, early_send, early_recv, nt, cv, fo, rest, sel, act_t,
    gu0, gu1, gu2, gd0, gd1, gd2,
    ru0, ru1, ru2, rd0, rd1, rd2,
    iu0, iu1, iu2, id0, id1, id2,
    su0, su1, su2, sd0, sd1, sd2,
    i2u0, i2u1, i2u2, i2d0, i2d1, i2d2,
    s2u0, s2u1, s2u2, s2d0, s2d1, s2d2,
    i3u0, i3u1, i3u2, i3d0, i3d1, i3d2,
    gg, gin,
    load_sem, own_sem, a2a_ssem, a2a_rsem, early_ssem, early_rsem, row_ssem, row_rsem, red_ssem, red_rsem, gain_ssem, gain_rsem,
):
    grad = ((gu0, gu1, gu2), (gd0, gd1, gd2))
    rly = ((ru0, ru1, ru2), (rd0, rd1, rd2))
    inb = ((iu0, iu1, iu2), (id0, id1, id2))
    s1 = ((su0, su1, su2), (sd0, sd1, sd2))
    in2 = ((i2u0, i2u1, i2u2), (i2d0, i2d1, i2d2))
    s2 = ((s2u0, s2u1, s2u2), (s2d0, s2d1, s2d2))
    in3 = ((i3u0, i3u1, i3u2), (i3d0, i3d1, i3d2))

    sec = lax.axis_index("section")
    me = lax.axis_index("peer")
    pos = (me // 16, lax.rem(me // 4, 4), lax.rem(me, 4))
    weight = (16, 4, 1)

    def along(axis, step):
        there = mod4(pos[axis] + step)
        return (sec, me + (there - pos[axis]) * weight[axis])

    partner = (1 - sec, me)

    def half_load(h):
        cols = pl.ds(h * HALF, HALF)
        return pltpu.make_async_copy(cot_hbm.at[0, :, cols], cot_v.at[:, cols], load_sem.at[h])

    wd_load = pltpu.make_async_copy(wd_hbm.at[0], wd_v, load_sem.at[2])
    wu_load = pltpu.make_async_copy(wu_hbm.at[0], wu_v, load_sem.at[3])
    x_load = pltpu.make_async_copy(x_hbm, x_v, load_sem.at[4])
    gain_load = pltpu.make_async_copy(gain_hbm, gain_ref, load_sem.at[5])
    routes_load = pltpu.make_async_copy(routes_hbm, routes_ref, load_sem.at[6])
    counts_load = pltpu.make_async_copy(counts_hbm, counts_ref, load_sem.at[7])
    barrier = pltpu.get_barrier_semaphore()

    def cols_of(c):
        return pl.ds(pl.multiple_of(c * CH, CH), CH)

    def blocks(quarters, width):
        o_i = lax.broadcasted_iota(jnp.int32, (SLOTS, SLOTS), 0)
        i_i = lax.broadcasted_iota(jnp.int32, (SLOTS, SLOTS), 1)
        perm = jnp.where(i_i == (o_i & 3) * 64 + (o_i >> 2), 1.0, 0.0).astype(BF)
        moved = jnp.dot(perm, jnp.concatenate(quarters, axis=0), preferred_element_type=F32)
        return moved.astype(BF).reshape(16, 16, width)

    def arrange(h):
        for g in range(4):
            rows = slice(g * 64, (g + 1) * 64)
            starts = [h * HALF + j * QUART for j in range(4)]
            a2a_send[g * 16:(g + 1) * 16] = blocks([cot_v[rows, lo:lo + QUART] for lo in starts], QUART)

    def peer_at(i):
        i2, i1, i0 = i // 16, lax.rem(i // 4, 4), lax.rem(i, 4)
        return mod4(pos[0] + i2 + i0) * 16 + mod4(pos[1] + i1 + i0) * 4 + mod4(pos[2] + i0)

    def send_rows(h):
        def send(i, carry):
            dst = peer_at(i)
            rcopy(
                a2a_send.at[dst], a2a_recv.at[h, i], a2a_ssem, a2a_rsem.at[h, i // GROUP], (1, dst)
            ).start()
            return carry

        lax.fori_loop(h, N_PEER, send, 0)

    def arrange_early():
        def body(c, acc):
            return acc + lax.dot_general(
                cot_v[:, cols_of(c)], wu_v[:, cols_of(c)], INNER, preferred_element_type=F32
            )

        d_slot = lax.fori_loop(0, N_CH, body, jnp.zeros((SLOTS, R), F32), unroll=UNROLL)
        high = d_slot.astype(BF)
        low = (d_slot - high.astype(F32)).astype(BF)
        for g in range(4):
            rows = slice(g * 64, (g + 1) * 64)
            early_send[g * 16:(g + 1) * 16] = blocks(
                [part[rows, lo:lo + 128] for part in (high, low) for lo in (0, 128)], 128
            )

    def send_early():
        pltpu.make_async_copy(early_send.at[me], early_recv.at[0], own_sem.at[0]).start()

        def send(i, carry):
            dst = peer_at(i)
            rcopy(early_send.at[dst], early_recv.at[i], early_ssem, early_rsem, (1, dst)).start()
            return carry

        lax.fori_loop(1, N_PEER, send, 0)

    def row_wait(ref, c):
        return rcopy(ref.at[:, cols_of(c)], ref.at[:, cols_of(c)], row_ssem.at[c], row_rsem.at[c], partner)

    def scaled(c):
        return (x_v[:, cols_of(c)].astype(F32) * gain_ref[:, cols_of(c)]).astype(BF)

    def turn_rows(c, carry):
        half = pl.ds(pl.multiple_of(lax.rem(c, 2) * 8, 8), 8)
        nt[c // 2, half] = scaled(c).T.reshape(8, 80, ROWS)
        return carry

    def forward(arriving):
        def down(c, carry):
            raw, total = carry
            if arriving:
                row_wait(x_v, c).wait_recv()
            xf = x_v[:, cols_of(c)].astype(F32)
            total = total + jnp.sum(xf * xf, axis=1, keepdims=True)
            return raw + jnp.dot(scaled(c), wd_v[cols_of(c), :], preferred_element_type=F32), total

        start = jnp.zeros((ROWS, R), F32), jnp.zeros((ROWS, 1), F32)
        raw, total = lax.fori_loop(0, N_CH, down, start, unroll=UNROLL)
        inv = lax.rsqrt(total / D + rms_eps)
        hidden = raw * inv
        gate = jax.nn.sigmoid(hidden)
        active = (hidden * gate).astype(BF)
        act_t[...] = active.T
        return inv, hidden, gate, active

    def choose():
        dest = routes_ref[...]
        live = lax.broadcasted_iota(jnp.int32, (1, ROWS), 1) < counts_ref[...]
        lane = lax.broadcasted_iota(jnp.int32, (ROWS, ROWS), 1)
        row = lax.broadcasted_iota(jnp.int32, (ROWS, ROWS), 0)
        named = jnp.where((row == dest) & live, 1.0, 0.0)
        before = jnp.where(row < lane, 1.0, 0.0).astype(BF)
        rank = jnp.dot(named.astype(BF), before, preferred_element_type=F32)
        nth = jnp.sum(named * rank, axis=0, keepdims=True)
        z = (pos[2] + 4 - (dest & 3)) & 3
        x = (pos[1] + 8 - ((dest >> 2) & 3) - z) & 3
        y = (pos[0] + 8 - (dest >> 4) - z) & 3
        turn = y * 16 + x * 4 + z
        across = jnp.where(live, turn.astype(F32) * 16.0 + nth * 4.0, -16.0)
        place = jnp.sum(jnp.where(row == lane, across, 0.0), axis=1, keepdims=True)
        column = lax.broadcasted_iota(jnp.int32, (ROWS, N_PEER * 16), 1).astype(F32)
        for j in range(4):
            sel[j * ROWS:(j + 1) * ROWS, :] = jnp.where(column == place + float(j), 1.0, 0.0).astype(BF)

    def early_active():
        pltpu.make_async_copy(early_send.at[me], early_recv.at[0], own_sem.at[0]).wait()
        others = early_recv.at[pl.ds(1, N_PEER - 1)]
        rcopy(others, others, early_ssem, early_rsem, partner).wait_recv()
        got = jnp.dot(
            sel[...], early_recv[...].reshape(N_PEER * 16, 128), preferred_element_type=F32
        ).reshape(4, ROWS, 128)
        return jnp.concatenate([got[0] + got[2], got[1] + got[3]], axis=1)

    def pick(g):
        group = pl.ds(g * GROUP, GROUP)
        for h in range(2):
            landed = a2a_recv.at[h, group]
            if h == 1 and g == 0:
                pltpu.make_async_copy(a2a_send.at[me], a2a_recv.at[1, 0], own_sem.at[1]).wait()
                landed = a2a_recv.at[1, pl.ds(1, GROUP - 1)]
            rcopy(landed, landed, a2a_ssem, a2a_rsem.at[h, g], partner).wait_recv()
            picked = jnp.dot(
                sel[:, g * GROUP * 16:(g + 1) * GROUP * 16],
                a2a_recv[h, group].reshape(GROUP * 16, QUART),
                preferred_element_type=F32,
            ).astype(BF)
            for j in range(4):
                cols = pl.ds((h * 4 + j) * CH, CH)
                part = picked[j * ROWS:(j + 1) * ROWS, :]
                if g > 0:
                    part = cv[:, cols] + part
                cv[:, cols] = part
                if g == N_GROUP - 1:
                    out_rows[:, cols] = (part.astype(F32) + rest[:, cols]).astype(BF)
                    rcopy(
                        out_rows.at[:, cols], cv.at[:, cols],
                        row_ssem.at[h * 4 + j], row_rsem.at[h * 4 + j], partner,
                    ).start()

    def out_at(t, k, a, b, c):
        if t == 0:
            cols = pl.ds(pl.multiple_of(a * ACOL + UP_OFF[k], 128), UP_W[k])
            return out_up.at[b, c, :, cols]
        return out_dn.at[a, b, c, pl.ds(DN_OFF[k], DN_H[k]), :]

    every = pl.ds(0, RING)
    lower, upper = pl.ds(0, 2), pl.ds(2, 2)

    def sems(t, k, i):
        return red_ssem.at[t, k], red_rsem.at[t, k, i]

    def ship(src, dst, t, k, i, device):
        rcopy(src, dst, *sems(t, k, i), device).start()

    def here(dst, t, k, i):
        wait_recv(dst, sems(t, k, i), partner)

    def first_axis(k):
        return pos[ORDER[k][0]]

    def sides(k):
        axis = ORDER[k][0]
        return along(axis, -1), along(axis, 1)

    def stage1_send(t):
        for k in range(3):
            g, left, right = grad[t][k], *sides(k)
            ship(g.at[2, lower], rly[t][k].at[0], t, k, 0, right)
            ship(g.at[2, upper], rly[t][k].at[1], t, k, 1, left)
            ship(g.at[1, upper], inb[t][k].at[0, upper], t, k, 2, right)
            ship(g.at[3, lower], inb[t][k].at[1, lower], t, k, 2, left)

    def stage1_merge(t):
        for k in range(3):
            g, left, right = grad[t][k], *sides(k)
            here(rly[t][k].at[0], t, k, 0)
            g[1, 0:2] = (g[1, 0:2].astype(F32) + rly[t][k][0].astype(F32)).astype(BF)
            ship(g.at[1, lower], inb[t][k].at[0, lower], t, k, 2, right)
            here(rly[t][k].at[1], t, k, 1)
            g[3, 2:4] = (g[3, 2:4].astype(F32) + rly[t][k][1].astype(F32)).astype(BF)
            ship(g.at[3, upper], inb[t][k].at[1, upper], t, k, 2, left)

    def stage2_send(t):
        for k in range(3):
            g, box, part = grad[t][k], inb[t][k], s1[t][k]
            here(box, t, k, 2)

            def add(b, carry, g=g, box=box, part=part):
                part[b] = (g[0, b].astype(F32) + box[0, b].astype(F32) + box[1, b].astype(F32)).astype(BF)
                return carry

            lax.fori_loop(0, RING, add, 0)
            axis = ORDER[k][1]
            for step in range(1, 4):
                ship(part.at[mod4(pos[axis] + step)], in2[t][k].at[step - 1], t, k, 3, along(axis, step))

    def line_sum(t, k):
        box = in2[t][k]
        here(box, t, k, 3)
        mine = s1[t][k][pos[ORDER[k][1]]].astype(F32)
        return (mine + box[0].astype(F32) + box[1].astype(F32) + box[2].astype(F32)).astype(BF)

    def stage3_send(t):
        @pl.when(sec == 0)
        def _():
            for k in range(3):
                axis = ORDER[k][2]
                part = in3[t][k].at[pos[axis]]
                part[...] = line_sum(t, k)
                for step in range(1, 4):
                    ship(part, part, t, k, 4, along(axis, step))

        @pl.when(sec == 1)
        def _():
            for k in range(3):
                axis = ORDER[k][2]
                part = s2[t][k]
                part[...] = line_sum(t, k)
                for step in range(1, 4):
                    ship(part.at[mod4(pos[axis] + step)], in3[t][k].at[0, step - 1], t, k, 4, along(axis, step))

    def gather1_send(t):
        @pl.when(sec == 1)
        def _():
            for k in range(3):
                a, b, c = (pos[axis] for axis in ORDER[k])
                box = in3[t][k].at[0]
                here(box.at[0:3], t, k, 4)
                mine = s2[t][k][c].astype(F32)
                whole = mine + box[0].astype(F32) + box[1].astype(F32) + box[2].astype(F32)
                piece = out_at(t, k, a, b, c)
                piece[...] = (whole * FACTOR).astype(BF)
                for step in range(1, 4):
                    ship(piece, piece, t, k, 5, along(ORDER[k][2], step))

    def gather2_send(t):
        for k in range(3):
            a, b, _ = (pos[axis] for axis in ORDER[k])
            box = in3[t][k]
            mine = out_at(t, k, a, b, every)

            @pl.when(sec == 0)
            def _(k=k, box=box, mine=mine):
                here(box.at[0:3], t, k, 4)
                whole = box[0].astype(F32) + box[1].astype(F32) + box[2].astype(F32) + box[3].astype(F32)
                mine[...] = (whole * FACTOR).astype(BF)

            @pl.when(sec == 1)
            def _(k=k, box=box):
                here(box.at[0, 0:3], t, k, 5)

            axis = ORDER[k][1]
            for step in range(1, 4):
                ship(mine, mine, t, k, 6, along(axis, step))

    def gather3_send(t):
        for k in range(3):
            here(in2[t][k], t, k, 6)
            left, right = sides(k)
            a = first_axis(k)
            low, high = out_at(t, k, a, lower, every), out_at(t, k, a, upper, every)
            ship(low, low, t, k, 7, right)
            ship(high, high, t, k, 8, left)
            ship(high, high, t, k, 9, right)
            ship(low, low, t, k, 9, left)

    def relay_send(t):
        for k in range(3):
            a = first_axis(k)
            left, right = sides(k)
            part = out_at(t, k, mod4(a - 1), lower, every)
            here(part, t, k, 7)
            ship(part, part, t, k, 9, right)
            part = out_at(t, k, mod4(a + 1), upper, every)
            here(part, t, k, 8)
            ship(part, part, t, k, 9, left)

    def finish(t):
        for k in range(3):
            here(inb[t][k], t, k, 9)
            g = grad[t][k]

            @pl.when(sec == 0)
            def _(k=k, g=g):
                for sent in (g, g, g.at[0, 0]):
                    wait_send(sent, sems(t, k, 0), partner)

            @pl.when(sec == 1)
            def _(k=k, g=g):
                for sent in (g, g.at[0:3], g.at[3, 0:3], g.at[3, 3, 0:2]):
                    wait_send(sent, sems(t, k, 0), partner)

    def make_up():
        def body(j, carry):
            for k in range(3):
                a = mod4(first_axis(k) + j)
                cols = pl.ds(pl.multiple_of(a * ACOL + UP_OFF[k], 128), UP_W[k])
                g = jnp.dot(act_t[...], cv[:, cols], preferred_element_type=F32)
                grad[0][k][j] = g.astype(BF).reshape(4, 4, 16, UP_W[k])
            return carry

        lax.fori_loop(0, RING, body, 0, unroll=UNROLL)
        stage1_send(0)

    def make_down(d_hidden, inv):
        d_scaled = (d_hidden * inv).astype(BF)

        def body(j, carry):
            for k in range(3):
                a = mod4(first_axis(k) + j)
                h = DN_H[k]
                lhs = nt[a, :, DN_OFF[k]:DN_OFF[k] + h, :].reshape(16 * h, ROWS)
                g = jnp.dot(lhs, d_scaled, preferred_element_type=F32)
                grad[1][k][j] = g.astype(BF).reshape(4, 4, h, R)
            return carry

        lax.fori_loop(0, RING, body, 0, unroll=UNROLL)
        stage1_send(1)

    def hidden_grad(d_active, hidden, gate):
        return d_active * gate * (1.0 + hidden * (1.0 - gate))

    def row_pass(d_hidden, hidden, inv, last):
        d_hidden = d_hidden.astype(BF)
        mean = jnp.sum(d_hidden.astype(F32) * hidden, axis=1, keepdims=True) / D

        def body(c, carry):
            cols = cols_of(c)
            d_normed = lax.dot_general(d_hidden, wd_v[cols, :], INNER, preferred_element_type=F32)
            x_hat = x_v[:, cols].astype(F32) * inv
            gg[0, :, cols] = jnp.sum(d_normed * x_hat, axis=0, keepdims=True)
            change = inv * (d_normed * gain_ref[:, cols] - x_hat * mean)
            if last:
                out_rows[:, cols] = (cv[:, cols].astype(F32) + change).astype(BF)
            else:
                rest[:, cols] = change
            return carry

        lax.fori_loop(0, N_CH, body, 0, unroll=UNROLL)

    @pl.when(sec == 1)
    def _():
        half_load(1).start()
        half_load(0).start()
        wu_load.start()

        def greet(i, carry):
            pl.semaphore_signal(barrier, inc=1, device_id=(0, peer_at(i)), device_id_type=MESH)
            return carry

        lax.fori_loop(0, N_PEER, greet, 0)
        routes_load.start()
        counts_load.start()
        gain_load.start()
        wd_load.start()
        half_load(1).wait()
        arrange(1)
        half_load(0).wait()
        wu_load.wait()
        arrange_early()
        pl.semaphore_wait(barrier, 1)
        send_early()
        pltpu.make_async_copy(a2a_send.at[me], a2a_recv.at[1, 0], own_sem.at[1]).start()
        send_rows(1)
        routes_load.wait()
        counts_load.wait()
        choose()
        gain_load.wait()
        wd_load.wait()
        inv, hidden, gate, _ = forward(True)
        lax.fori_loop(0, N_CH, turn_rows, 0, unroll=UNROLL)
        d_hidden = hidden_grad(early_active(), hidden, gate)
        make_down(d_hidden, inv)
        pick(0)
        pick(1)
        row_pass(d_hidden, hidden, inv, False)
        pick(2)
        pick(3)
        make_up()

    @pl.when(sec == 0)
    def _():
        half_load(0).start()
        x_load.start()
        gain_load.start()
        wd_load.start()
        wu_load.start()
        for axis in range(3):
            for step in range(1, 4):
                pl.semaphore_signal(barrier, inc=1, device_id=along(axis, step), device_id_type=MESH)
        half_load(0).wait()
        arrange(0)
        pl.semaphore_wait(barrier, N_PEER + 9)
        pl.semaphore_signal(barrier, inc=1, device_id=partner, device_id_type=MESH)
        send_rows(0)
        x_load.wait()
        gain_load.wait()
        wd_load.wait()
        inv, hidden, gate, active = forward(False)
        wu_load.wait()

        def up(c, carry):
            y = jnp.dot(active, wu_v[:, cols_of(c)], preferred_element_type=F32)
            fo[:, cols_of(c)] = (x_v[:, cols_of(c)].astype(F32) + y).astype(BF)
            rcopy(
                fo.at[:, cols_of(c)], x_v.at[:, cols_of(c)], row_ssem.at[c], row_rsem.at[c], partner
            ).start()
            return carry

        lax.fori_loop(0, N_CH, up, 0, unroll=UNROLL)
        lax.fori_loop(0, N_CH, turn_rows, 0, unroll=UNROLL)

        def body(c, acc):
            row_wait(cv, c).wait_recv()
            return acc + lax.dot_general(
                cv[:, cols_of(c)], wu_v[:, cols_of(c)], INNER, preferred_element_type=F32
            )

        d_active = lax.fori_loop(0, N_CH, body, jnp.zeros((ROWS, R), F32), unroll=UNROLL)
        d_hidden = hidden_grad(d_active, hidden, gate)
        make_down(d_hidden, inv)
        make_up()
        row_pass(d_hidden, hidden, inv, True)

    def gain_send(stage):
        axis = 2 - stage
        for step in range(1, 4):
            rcopy(
                gg.at[stage], gin.at[stage, step - 1], gain_ssem, gain_rsem.at[stage], along(axis, step)
            ).start()

    def gain_add(stage):
        wait_recv(gin.at[stage], (gain_ssem, gain_rsem.at[stage]), partner)
        gg[stage + 1] = gg[stage] + gin[stage, 0] + gin[stage, 1] + gin[stage, 2]

    both = (1, 0)
    for t in both:
        stage1_merge(t)
    for t in both:
        stage2_send(t)
    gain_send(0)
    for t in both:
        stage3_send(t)
    gain_add(0)
    gain_send(1)
    for t in both:
        gather1_send(t)
    for t in both:
        gather2_send(t)
    gain_add(1)
    gain_send(2)
    for t in both:
        gather3_send(t)
    for t in both:
        relay_send(t)
    gain_add(2)
    out_gain[...] = (gg[3] * FACTOR).astype(BF)
    for t in both:
        finish(t)

    wait_send(gin, (gain_ssem, gain_rsem.at[0]), partner)

    @pl.when(sec == 0)
    def _():
        rcopy(a2a_send, a2a_send, a2a_ssem, early_rsem, partner).wait_send()

        def sent(c, carry):
            row_wait(fo, c).wait_send()
            return carry

        lax.fori_loop(0, N_CH, sent, 0)

    @pl.when(sec == 1)
    def _():
        for sent_from, sem in ((a2a_send, a2a_ssem), (early_send, early_ssem)):
            others = sent_from.at[pl.ds(0, N_PEER - 1)]
            rcopy(others, others, sem, early_rsem, partner).wait_send()

        def sent(c, carry):
            row_wait(out_rows, c).wait_send()
            return carry

        lax.fori_loop(0, N_CH, sent, 0)


def both_kinds(lead):
    ups = [pltpu.VMEM((*lead, 16, w), BF) for w in UP_W]
    downs = [pltpu.VMEM((*lead, h, R), BF) for h in DN_H]
    return ups + downs


def write_out(*refs):
    n = (len(refs) - 1) // 2
    sem = refs[-1]
    copies = [pltpu.make_async_copy(refs[i], refs[n + i], sem.at[i]) for i in range(n)]
    for copy in copies:
        copy.start()
    for copy in copies:
        copy.wait()


def stay(operand):
    return pltpu.with_memory_space_constraint(operand, pltpu.HBM)


def shards(inputs, routes, counts, cotangent, gain_vector, w_down, w_up):
    hbm = pl.BlockSpec(memory_space=pltpu.HBM)
    vmem = pl.BlockSpec(memory_space=pltpu.VMEM)
    anywhere = pl.BlockSpec(memory_space=pl.ANY)
    dma = pltpu.SemaphoreType.DMA
    scratch = [
        pltpu.VMEM((ROWS, D), BF),
        pltpu.VMEM((1, ROWS), jnp.int32),
        pltpu.VMEM((1, 1), jnp.int32),
        pltpu.VMEM((1, D), F32),
        pltpu.VMEM((D, R), BF),
        pltpu.VMEM((R, D), BF),
        pltpu.VMEM((SLOTS, D), BF),
        pltpu.VMEM((N_PEER, 16, QUART), BF),
        pltpu.VMEM((2, N_PEER, 16, QUART), BF),
        pltpu.VMEM((N_PEER, 16, 128), BF),
        pltpu.VMEM((N_PEER, 16, 128), BF),
        pltpu.VMEM((RING, 16, 80, ROWS), BF),
        pltpu.VMEM((ROWS, D), BF),
        pltpu.VMEM((ROWS, D), BF),
        pltpu.VMEM((ROWS, D), F32),
        pltpu.VMEM((4 * ROWS, N_PEER * 16), BF),
        pltpu.VMEM((R, ROWS), BF),
    ]
    for lead in ((4, 4, 4), (2, 2, 4), (2, 4, 4), (4, 4), (3, 4), (4,), (4, 4)):
        scratch += both_kinds(lead)
    scratch += [
        pltpu.VMEM((4, 1, D), F32),
        pltpu.VMEM((3, 3, 1, D), F32),
        dma((8,)),
        dma((2,)),
        dma,
        dma((2, N_GROUP)),
        dma,
        dma,
        dma((N_CH,)),
        dma((N_CH,)),
        dma((2, 3)),
        dma((2, 3, 10)),
        dma,
        dma((3,)),
    ]
    shapes = [(1, D), (RING, RING, RING, 80, R), (RING, RING, 16, D), (ROWS, D)]
    made = pl.pallas_call(
        kernel,
        out_shape=[pltpu.VMEM(s, BF) for s in shapes],
        in_specs=[hbm, anywhere, anywhere, hbm, hbm, hbm, hbm],
        out_specs=[vmem] * 4,
        scratch_shapes=scratch,
        compiler_params=pltpu.CompilerParams(
            collective_id=0, has_side_effects=True, vmem_limit_bytes=44 * 2**20
        ),
    )(
        stay(inputs), stay(routes.reshape(1, ROWS)), counts.reshape(1, 1), stay(cotangent), stay(gain_vector),
        stay(w_down), stay(w_up),
    )
    gain, down, up, rows = pl.pallas_call(
        write_out,
        out_shape=[jax.ShapeDtypeStruct(s, BF) for s in shapes],
        in_specs=[vmem] * 4,
        out_specs=[hbm] * 4,
        scratch_shapes=[dma((4,))],
        compiler_params=pltpu.CompilerParams(vmem_limit_bytes=2**20),
    )(*made)
    return gain, down.reshape(1, D, R), up.reshape(1, R, D), rows[None]


def solution(mesh):
    in_specs = (
        P("peer", None),
        P("peer", None),
        P("peer"),
        P("peer", None, None),
        P("section", None),
        P("section", None, None),
        P("section", None, None),
    )
    out_specs = (
        P("section", None),
        P("section", None, None),
        P("section", None, None),
        P("section", "peer", None),
    )
    return jax.shard_map(shards, mesh=mesh, in_specs=in_specs, out_specs=out_specs, check_vma=False)
```
